128 devices in a mesh: gy: 16 (over z, y_lo, core), gx: 8 (over y_hi, x).
Axes of the slice: x: 4, y: 4 (y_hi: 2, y_lo: 2; y = y_hi * 2 + y_lo), z: 4, core: 2. Of those that a mesh axis runs over, the one named last changes fastest.
Arguments:
- fine: bfloat16 [128, 96, 768], P('gy', 'gx'), may hold values from -6 to 6
- class_table: bfloat16 [1000, 768], replicated, may hold values from -3 to 3
- label: int32 [1], replicated, may hold values from 0 to 999
- timestep: int32 [1], replicated, may hold values from 0 to 999
- windows: int32 [12], replicated, may hold values from 3 to 7, as said below
- fine_scale: float32 [12], replicated, may hold values from 4 to 400
- fine_qkv: bfloat16 [768, 2304], replicated, may hold values from -0.21875 to 0.21875
- fine_out: bfloat16 [768, 768], replicated, may hold values from -0.21875 to 0.21875
- merge_weight: bfloat16 [3072, 1536], P(('gy', 'gx')), may hold values from -0.109375 to 0.109375
- bottom_scale: float32 [12], replicated, may hold values from 4 to 400
- bottom_qkv: bfloat16 [1536, 2304], replicated, may hold values from -0.15625 to 0.15625
- bottom_out: bfloat16 [768, 1536], replicated, may hold values from -0.21875 to 0.21875
- split_weight: bfloat16 [1536, 3072], P(None, ('gy', 'gx')), may hold values from -0.15625 to 0.15625
- skip_mix: float32 [768], replicated, may hold values from 0.2 to 0.8
Outputs:
- mixed: bfloat16 [128, 96, 768], P('gy', 'gx')
The draws below stay inside these ranges and needn't reach their ends.
Inputs may be any that keep to these rules, and one draw needn't show every extreme that they name: `windows`: odd window sizes; some head has window 7.
All inputs are finite; a program needn't handle non-finite values.
Results may differ from the reference program's by a relative error of at most 0.034.
Values may be sent and summed in bfloat16 or wider, within the bound.
No kernel may reach another device: no remote copies, remote signals or barrier semaphores. Data moves between devices by JAX's collectives and lax.ppermute only.
A program may use at most 192 MiB of HBM per device.

```python
import math
import jax
import jax.numpy as jnp
from jax import lax

D = 768
DB = 1536
CLASSES = 1000
HEAD_DIM = 64
HB = 12
WIN = 7
HF = 12
AB = 768
GH = 128
GW = 96


def draw_windows(key, part):
    key = jax.random.fold_in(key, 7)
    first, second = jax.random.split(key)
    radius = jax.random.randint(first, (HF,), 1, 4)
    place = jax.random.randint(second, (), 0, HF)
    radius = jnp.where(jnp.arange(HF) == place, 3, radius)
    return (2 * radius + 1).astype(jnp.int32)


def scale_draw(key, count, low, high):
    return jnp.exp(jax.random.uniform(key, (count,), jnp.float32, math.log(low), math.log(high)))


def draw_fine_scale(key, part):
    key = jax.random.fold_in(key, 11)
    return scale_draw(key, HF, 8.0, 32.0)


def draw_bottom_scale(key, part):
    key = jax.random.fold_in(key, 13)
    return scale_draw(key, HB, 24.0, 96.0)


def shard_levels(stream_key, shape, cuts, smallest, high):
    def one(axis_at, parts):
        heights = jax.random.uniform(jax.random.fold_in(jax.random.fold_in(stream_key, 6), axis_at), (parts,), jnp.float32, smallest / len(cuts), high / len(cuts))
        return jnp.repeat(jnp.exp(heights), shape[axis_at] // parts).reshape((-1,) + (1,) * (len(shape) - axis_at - 1))

    level = one(*cuts[0])
    for cut in cuts[1:]:
        level = level * one(*cut)
    return level


def noise(stream_key, extent, scale, most, shards=(), held_as=jnp.bfloat16):
    factor_of = shard_levels(stream_key, extent, shards, -0.22, 0.18) if shards else 1.0
    values = jax.random.normal(stream_key, extent, jnp.float32) * scale * factor_of
    return jnp.minimum(jnp.maximum(values, -most), most).astype(held_as)


def setup_inputs(seed: int = 0) -> dict:
    arg_keys = jax.random.split(jax.random.key(seed), 15)
    return {
        "fine": noise(arg_keys[0], (GH, GW, D), 1.0, 6.0, ((0, 16), (1, 8))),
        "class_table": noise(arg_keys[1], (CLASSES, D), 0.5, 3.0),
        "label": jax.random.randint(arg_keys[2], (1,), 0, CLASSES).astype(jnp.int32),
        "timestep": jax.random.randint(arg_keys[3], (1,), 0, 1000).astype(jnp.int32),
        "windows": draw_windows(jax.random.fold_in(arg_keys[14], 71), 0),
        "fine_scale": draw_fine_scale(jax.random.fold_in(arg_keys[14], 71), 0),
        "fine_qkv": noise(arg_keys[6], (D, 3 * D), D ** -0.5, 0.21875),
        "fine_out": noise(arg_keys[7], (D, D), D ** -0.5, 0.21875),
        "merge_weight": noise(arg_keys[8], (4 * D, DB), (4 * D) ** -0.5, 0.109375, ((0, 128),)),
        "bottom_scale": draw_bottom_scale(jax.random.fold_in(arg_keys[14], 71), 0),
        "bottom_qkv": noise(arg_keys[10], (DB, 3 * AB), DB ** -0.5, 0.15625),
        "bottom_out": noise(arg_keys[11], (AB, DB), AB ** -0.5, 0.21875),
        "split_weight": noise(arg_keys[12], (DB, 4 * D), DB ** -0.5, 0.15625, ((1, 128),)),
        "skip_mix": jnp.clip(jax.random.uniform(arg_keys[13], (D,), jnp.float32, 0.2, 0.8), 0.2, 0.8),
    }


EPS = 1e-06

def time_features(step, width):
    half = width // 2
    freqs = jnp.exp(-math.log(10000.0) * jnp.arange(half, dtype=jnp.float32) / half)
    angles = step[0].astype(jnp.float32) * freqs
    return jnp.concatenate([jnp.cos(angles), jnp.sin(angles)])

def rms_scale(values, gain):
    return values * lax.rsqrt(lax.optimization_barrier(jnp.mean(values * values, axis=-1, keepdims=True)) + EPS) * gain

def unit_heads(values):
    return values * lax.rsqrt(lax.optimization_barrier(jnp.sum(values * values, axis=-1, keepdims=True)) + EPS)

def neighbour_attention(queries, padded, row_start, col_start, rows_all, cols_all, windows, scales):
    height, width, heads, depth = queries.shape
    reach = WIN // 2
    radius = (windows - 1) // 2
    row_pos = row_start + jnp.arange(height, dtype=jnp.int32)
    col_pos = col_start + jnp.arange(width, dtype=jnp.int32)
    scored = []
    for row_off in range(WIN):
        for col_off in range(WIN):
            window = padded[row_off:row_off + height, col_off:col_off + width, :heads * depth]
            keys = window.reshape(height, width, heads, depth).astype(jnp.float32)
            score = scales * lax.optimization_barrier(jnp.sum(queries * keys, axis=-1))
            shift_row = row_off - reach
            shift_col = col_off - reach
            rows_in = (row_pos + shift_row >= 0) & (row_pos + shift_row < rows_all)
            cols_in = (col_pos + shift_col >= 0) & (col_pos + shift_col < cols_all)
            allowed = (abs(shift_row) <= radius) & (abs(shift_col) <= radius)
            valid = rows_in[:, None, None] & cols_in[None, :, None] & allowed[None, None, :]
            scored.append(jnp.where(valid, score, -jnp.inf))
    stacked = jnp.stack(scored, axis=-1)
    highest = lax.optimization_barrier(jnp.max(stacked, axis=-1, keepdims=True))
    expd = jnp.exp(stacked - highest)
    weights = expd / lax.optimization_barrier(jnp.sum(expd, axis=-1, keepdims=True))
    output = jnp.zeros((height, width, heads, depth), jnp.float32)
    for row_off in range(WIN):
        for col_off in range(WIN):
            window = padded[row_off:row_off + height, col_off:col_off + width, heads * depth:]
            values = window.reshape(height, width, heads, depth).astype(jnp.float32)
            output = output + weights[..., row_off * WIN + col_off, None] * values
    return output.reshape(height, width, heads * depth)

def merge_tokens(stream):
    height, width, depth = stream.shape
    blocks = stream.reshape(height // 2, 2, width // 2, 2, depth).transpose(0, 2, 1, 3, 4)
    return blocks.reshape(height // 2 * (width // 2), 4 * depth)

def split_tokens(split, height, width):
    depth = split.shape[1] // 4
    blocks = split.reshape(height // 2, width // 2, 2, 2, depth).transpose(0, 2, 1, 3, 4)
    return blocks.reshape(height, width, depth)

def fine_section(fine, class_table, label, timestep):
    width_feat = fine.shape[2]
    row = lax.dynamic_slice_in_dim(class_table, label[0], 1, 0)[0].astype(jnp.float32)
    cond = row + time_features(timestep, width_feat)
    gain = 1.0 + 0.5 * cond
    xfull = fine.astype(jnp.float32)
    return (xfull, rms_scale(xfull, gain).astype(jnp.bfloat16))

def one_head(inputs):
    queries, keys, values, scale = inputs
    score = scale * jnp.dot(queries, keys.astype(jnp.float32).T, precision=lax.Precision.HIGHEST)
    highest = lax.optimization_barrier(jnp.max(score, axis=-1, keepdims=True))
    expd = jnp.exp(score - highest)
    weights = expd / lax.optimization_barrier(jnp.sum(expd, axis=-1, keepdims=True))
    return jnp.dot(weights, values.astype(jnp.float32), precision=lax.Precision.HIGHEST)

def reference(fine, class_table, label, timestep, windows, fine_scale, fine_qkv, fine_out, merge_weight, bottom_scale, bottom_qkv, bottom_out, split_weight, skip_mix):
    height, width, depth = fine.shape
    heads = depth // HEAD_DIM
    xfull, normed = fine_section(fine, class_table, label, timestep)
    proj = jnp.dot(normed.reshape(-1, depth), fine_qkv, preferred_element_type=jnp.float32)
    queries = unit_heads(proj[:, :depth].reshape(height, width, heads, HEAD_DIM))
    keys = unit_heads(proj[:, depth:2 * depth].reshape(height, width, heads, HEAD_DIM))
    keys = keys.astype(jnp.bfloat16).reshape(height, width, depth)
    values = proj[:, 2 * depth:].astype(jnp.bfloat16).reshape(height, width, depth)
    packed = jnp.concatenate([keys, values], axis=-1)
    reach = WIN // 2
    padded = jnp.pad(packed, ((reach, reach), (reach, reach), (0, 0)))
    attended = neighbour_attention(queries, padded, 0, 0, height, width, windows, fine_scale).astype(jnp.bfloat16)
    update = jnp.dot(attended.reshape(-1, depth), fine_out, preferred_element_type=jnp.float32)
    stream = (xfull + update.reshape(height, width, depth)).astype(jnp.bfloat16)
    merged = merge_tokens(stream)
    bottom = jnp.dot(merged, merge_weight, preferred_element_type=jnp.float32).astype(jnp.bfloat16)
    bfull = bottom.astype(jnp.float32)
    bnormed = rms_scale(bfull, 1.0).astype(jnp.bfloat16)
    bproj = jnp.dot(bnormed, bottom_qkv, preferred_element_type=jnp.float32)
    count = bproj.shape[0]
    bheads = bottom_scale.shape[0]
    battn = bheads * HEAD_DIM
    bquery = unit_heads(bproj[:, :battn].reshape(count, bheads, HEAD_DIM))
    bkey = unit_heads(bproj[:, battn:2 * battn].reshape(count, bheads, HEAD_DIM)).astype(jnp.bfloat16)
    bvalue = bproj[:, 2 * battn:].reshape(count, bheads, HEAD_DIM).astype(jnp.bfloat16)
    per_head = lax.map(one_head, (bquery.transpose(1, 0, 2), bkey.transpose(1, 0, 2), bvalue.transpose(1, 0, 2), bottom_scale))
    batt = per_head.transpose(1, 0, 2).reshape(count, battn).astype(jnp.bfloat16)
    bstream = (bfull + jnp.dot(batt, bottom_out, preferred_element_type=jnp.float32)).astype(jnp.bfloat16)
    split = jnp.dot(bstream, split_weight, preferred_element_type=jnp.float32)
    upward = split_tokens(split, height, width)
    sfull = stream.astype(jnp.float32)
    return (sfull + skip_mix * (upward - sfull)).astype(jnp.bfloat16)
```

```python
import math

import jax
import jax.numpy as jnp
import numpy as np
from jax import lax
from jax.experimental import pallas as pl
from jax.experimental.pallas import tpu as pltpu
from jax.sharding import Mesh, PartitionSpec as P

HEAD_DIM = 64
WIN = 7
REACH = WIN // 2
EPS = 1e-06
ROWS, COLS = 8, 12
OWN = ROWS * COLS
TOKENS = OWN // 4
KEYS = 256
FAR = 1000
BF16 = jnp.bfloat16
F32 = jnp.float32

ALL = ("z", "yl", "c", "yh", "x")
GY = ("z", "yl", "c")
GX = ("yh", "x")
ZY = ("z", "yl", "yh")
NX = 4

VMEM_LIMIT = 40 * 2**20


def key_places():
    places = []
    for s in range(4):
        for t in range(TOKENS):
            places.append((2 * (t // 6) + s // 2, 2 * (t % 6) + s % 2))
    for r in (-3, -2, -1, 8, 9, 10):
        for c in range(COLS):
            places.append((r, c))
    for cols in ((-3, -2, -1), (12, 13, 14)):
        for r in range(-3, ROWS + 3):
            for c in cols:
                places.append((r, c))
    places += [(FAR, FAR)] * (KEYS - len(places))
    return np.array(places, np.int32)


PLACES = key_places()


def own_to_grid():
    matrix = np.zeros((16 * ROWS, OWN), np.float32)
    for i in range(OWN):
        r, c = PLACES[i]
        matrix[16 * r + c, i] = 1.0
    return matrix


def block_ones():
    return np.kron(np.eye(4), np.ones((HEAD_DIM, HEAD_DIM))).astype(np.float32)


def dot(a, b):
    return jnp.dot(a, b, preferred_element_type=F32)


def dot_t(a, b):
    return lax.dot_general(a, b, (((1,), (1,)), ((), ())), preferred_element_type=F32)


def split_hi_lo(values):
    hi = values.astype(BF16)
    lo = (values - hi.astype(F32)).astype(BF16)
    return hi, lo


def unit_quad(values, ones):
    hi, lo = split_hi_lo(values * values)
    total = dot(hi, ones) + dot(lo, ones)
    return values * lax.rsqrt(total + EPS)


def full(shape):
    return pl.BlockSpec(memory_space=pltpu.VMEM)


def smem():
    return pl.BlockSpec(memory_space=pltpu.SMEM)


def call(body, out_shape, args, in_smem, scratch=(), flops=0, nbytes=0):
    return pl.pallas_call(
        body,
        out_shape=out_shape,
        in_specs=[smem() if i in in_smem else full(None) for i in range(len(args))],
        out_specs=jax.tree.map(lambda _: full(None), out_shape),
        scratch_shapes=list(scratch),
        compiler_params=pltpu.CompilerParams(vmem_limit_bytes=VMEM_LIMIT),
        cost_estimate=pl.CostEstimate(flops=flops, bytes_accessed=nbytes, transcendentals=0),
    )(*args)


def fine_kernel(
    start, windows, scales, own, halo, gain, key_place, query_place, ones, qkv, out_w,
    stream,
):
    width = own.shape[1]

    def normed(ref):
        x = ref[...].astype(F32)
        mean = jnp.mean(x * x, axis=-1, keepdims=True)
        return x, (x * lax.rsqrt(mean + EPS) * gain[...]).astype(BF16)

    x_own, n_own = normed(own)
    _, n_halo = normed(halo)
    n_all = jnp.concatenate([n_own, n_halo], axis=0)

    row_k, col_k = key_place[0:1, :], key_place[1:2, :]
    row_q, col_q = query_place[:, 0:1], query_place[:, 1:2]
    row_g, col_g = row_k + start[0], col_k + start[1]
    inside = (row_g >= 0) & (row_g < start[2]) & (col_g >= 0) & (col_g < start[3])
    apart = jnp.maximum(jnp.abs(row_k - row_q), jnp.abs(col_k - col_q))
    apart = jnp.where(inside, apart, FAR)
    lane = lax.broadcasted_iota(jnp.int32, (OWN, 256), 1) // HEAD_DIM

    update = jnp.zeros((OWN, width), F32)
    for quad in range(width // 256):
        at = quad * 256
        query = unit_quad(dot(n_own, qkv[:, at : at + 256]), ones[...])
        key = unit_quad(dot(n_all, qkv[:, width + at : width + at + 256]), ones[...]).astype(BF16)
        value = dot(n_all, qkv[:, 2 * width + at : 2 * width + at + 256]).astype(BF16)
        hi, lo = split_hi_lo(query)
        rows = [jnp.where(lane == h, hi, 0) for h in range(4)]
        rows += [jnp.where(lane == h, lo, 0) for h in range(4)]
        score = dot_t(jnp.concatenate(rows, axis=0), key)
        score = score[: 4 * OWN] + score[4 * OWN :]
        weights, totals = [], []
        for h in range(4):
            head = quad * 4 + h
            radius = (windows[head] - 1) // 2
            part = jnp.where(apart <= radius, scales[head] * score[h * OWN : (h + 1) * OWN], -jnp.inf)
            part = jnp.exp(part - jnp.max(part, axis=-1, keepdims=True))
            totals.append(jnp.sum(part, axis=-1, keepdims=True))
            weights.append(part.astype(BF16))
        mixed = dot(jnp.concatenate(weights, axis=0), value)
        att = jnp.zeros((OWN, 256), F32)
        for h in range(4):
            att = jnp.where(lane == h, mixed[h * OWN : (h + 1) * OWN] / totals[h], att)
        update = update + dot(att.astype(BF16), out_w[at : at + 256, :])
    result = x_own + update
    for s in range(4):
        stream[s] = result[s * TOKENS : (s + 1) * TOKENS].astype(BF16)


def merge_kernel(place, p0, p1, p2, p3, weight, bottom):
    width = p0.shape[2]
    acc = None
    for s in range(4):
        rows = jnp.concatenate([p[s].astype(F32) for p in (p0, p1, p2, p3)], axis=0).astype(BF16)
        term = dot(rows, weight[s * width : (s + 1) * width, :])
        acc = term if acc is None else acc + term
    for k in range(NX):
        bottom[lax.rem(place[0] + NX - k, NX)] = acc[k * TOKENS : (k + 1) * TOKENS].astype(BF16)


def project_kernel(place, p0, p1, p2, p3, ones, weight, bottom, query, pairs, whole):
    block = p0.shape[2]
    for k, p in enumerate((p0, p1, p2, p3)):
        at = pl.multiple_of(lax.rem(place[0] + NX - k, NX) * block, 128)
        rows = jnp.concatenate([p[i].astype(F32) for i in range(NX)], axis=0)
        whole[:, pl.ds(at, block)] = rows
    x = whole[...]
    bottom[...] = x.astype(BF16)
    mean = jnp.mean(x * x, axis=-1, keepdims=True)
    normed = (x * lax.rsqrt(mean + EPS)).astype(BF16)
    proj = dot(normed, weight[...])
    first = proj[:, :256]
    lane = lax.broadcasted_iota(jnp.int32, first.shape, 1)
    first = jnp.where(lane < 192, unit_quad(first, ones[...]), first)
    kv = jnp.concatenate([first, proj[:, 256:384]], axis=1).astype(BF16)
    for i in range(pairs.shape[0]):
        pairs[i] = kv
    query[...] = unit_quad(proj[:, 384:640], ones[...])


def attend_kernel(scales, place, query, near, far, out):
    lane = lax.broadcasted_iota(jnp.int32, query.shape, 1) // HEAD_DIM
    count = query.shape[0]
    q = query[...]
    hi, lo = split_hi_lo(q)
    rows = [jnp.where(lane == h, hi, 0) for h in range(3)]
    rows += [jnp.where(lane == h, lo, 0) for h in range(3)]
    rows = jnp.concatenate(rows, axis=0)
    scale = jnp.concatenate(
        [jnp.full((count, 1), scales[3 * place[0] + h], F32) for h in range(3)], axis=0
    )
    scores = []
    for ref in (near, far):
        score = dot_t(rows, ref[:, :256])
        scores.append(scale * (score[: 3 * count] + score[3 * count :]))
    highest = jnp.maximum(
        jnp.max(scores[0], axis=-1, keepdims=True), jnp.max(scores[1], axis=-1, keepdims=True)
    )
    total = jnp.zeros((3 * count, 1), F32)
    acc = jnp.zeros((3 * count, 256), F32)
    for score, ref in zip(scores, (near, far)):
        part = jnp.exp(score - highest)
        total = total + jnp.sum(part, axis=-1, keepdims=True)
        acc = acc + dot(part.astype(BF16), ref[:, 128:384])
    acc = acc / total
    att = jnp.zeros((count, 256), F32)
    for h in range(3):
        att = jnp.where(lane == h + 1, acc[h * count : (h + 1) * count], att)
    out[...] = att[:, 64:].astype(BF16)


def output_kernel(place, p0, p1, p2, p3, bottom, out_w, split_w, split):
    acc = bottom[...].astype(F32)
    block = p0.shape[1]
    for k, p in enumerate((p0, p1, p2, p3)):
        at = pl.multiple_of(lax.rem(place[0] + NX - k, NX) * block, 64)
        acc = acc + dot(p[...], out_w[pl.ds(at, block), :])
    result = dot_t(acc.astype(BF16), split_w[...])
    for i in range(NX):
        split[i] = result[i * TOKENS : (i + 1) * TOKENS].astype(BF16)


def mix_kernel(stream, upward, mix, matrix, out):
    s = jnp.concatenate([stream[i].astype(F32) for i in range(4)], axis=0)
    u = jnp.concatenate([upward[i].astype(F32) for i in range(4)], axis=0)
    mixed = (s + mix[...] * (u - s)).astype(BF16)
    grid = dot(matrix[...], mixed).astype(BF16)
    for r in range(ROWS):
        out[r] = grid[16 * r : 16 * r + COLS]


def time_features(step, width):
    half = width // 2
    freqs = jnp.exp(-math.log(10000.0) * jnp.arange(half, dtype=F32) / half)
    angles = step[0].astype(F32) * freqs
    return jnp.concatenate([jnp.cos(angles), jnp.sin(angles)])


def shift(x, axis, size, step):
    return lax.ppermute(x, axis, [(i, i + step) for i in range(size) if 0 <= i + step < size])


def gather_x(x):
    return [x] + [
        lax.ppermute(x, "x", [(i, (i + s) % NX) for i in range(NX)]) for s in range(1, NX)
    ]


def swap_core(x):
    return lax.ppermute(x, "c", [(0, 1), (1, 0)])


def merge_columns(merge_weight):
    rows, width = merge_weight.shape
    block = width // NX
    parts = jnp.stack([merge_weight[:, i * block : (i + 1) * block] for i in range(NX)])
    parts = jnp.broadcast_to(parts[None], (16, NX, rows, block)).reshape(16 * NX, rows, block)
    mine = lax.all_to_all(parts, ("z", "yl", "yh", "x"), 0, 0)
    other = swap_core(mine)
    c = lax.axis_index("c")
    first = jnp.where(c == 0, mine, other).reshape(8, 8, rows, block)
    second = jnp.where(c == 0, other, mine).reshape(8, 8, rows, block)
    return jnp.stack([first, second], axis=1).reshape(128 * rows, block)


def split_columns(split_weight):
    chunk = split_weight.T
    rows, depth = chunk.shape
    chunk = lax.ppermute(
        chunk, ("z", "x"), [(z * 4 + x, x * 4 + z) for z in range(4) for x in range(4)]
    )
    mine = lax.all_to_all(jnp.broadcast_to(chunk[None], (16, rows, depth)), ZY, 0, 0)
    other = swap_core(mine)
    c = lax.axis_index("c")
    first = jnp.where(c == 0, mine, other).reshape(4, 2, 2, rows, depth)
    second = jnp.where(c == 0, other, mine).reshape(4, 2, 2, rows, depth)
    whole = jnp.stack([first, second], axis=0)
    return whole.transpose(2, 0, 3, 1, 4, 5).reshape(32 * rows, depth)


def shards(
    fine,
    class_table,
    label,
    timestep,
    windows,
    fine_scale,
    fine_qkv,
    fine_out,
    merge_weight,
    bottom_scale,
    bottom_qkv,
    bottom_out,
    split_weight,
    skip_mix,
):
    height, width, depth = fine.shape
    up = shift(fine[height - REACH :], GY, 16, 1)
    down = shift(fine[:REACH], GY, 16, -1)
    tall_left = jnp.concatenate([up[:, :REACH], fine[:, :REACH], down[:, :REACH]], axis=0)
    tall_right = jnp.concatenate(
        [up[:, width - REACH :], fine[:, width - REACH :], down[:, width - REACH :]], axis=0
    )
    left = shift(tall_right.reshape(-1, depth), GX, 8, 1)
    right = shift(tall_left.reshape(-1, depth), GX, 8, -1)
    own = fine.reshape(height // 2, 2, width // 2, 2, depth).transpose(1, 3, 0, 2, 4)
    own = own.reshape(OWN, depth)
    halo = jnp.concatenate(
        [
            up.reshape(-1, depth),
            down.reshape(-1, depth),
            left,
            right,
            jnp.zeros((4, depth), BF16),
        ],
        axis=0,
    )
    row = lax.dynamic_slice_in_dim(class_table, label[0], 1, 0)[0].astype(F32)
    gain = (1.0 + 0.5 * (row + time_features(timestep, depth)))[None]
    start = jnp.stack(
        [
            lax.axis_index(GY) * height,
            lax.axis_index(GX) * width,
            jnp.int32(16 * height),
            jnp.int32(8 * width),
        ]
    ).astype(jnp.int32)
    ones = jnp.asarray(block_ones(), BF16)
    place = lax.axis_index("x").astype(jnp.int32)[None]

    merge_w = merge_columns(merge_weight)
    split_w = split_columns(split_weight)
    battn = bottom_out.shape[0]
    group = battn // NX
    deep = bottom_qkv.shape[0]
    at = lax.axis_index("x") * group
    picked = [
        lax.dynamic_slice_in_dim(bottom_qkv, part * battn + at, group, 1) for part in (1, 2, 0)
    ]
    qkv_w = jnp.concatenate(picked + [jnp.zeros((deep, 64), BF16)], axis=1)

    stream = call(
        fine_kernel,
        jax.ShapeDtypeStruct((4, TOKENS, depth), BF16),
        [
            start,
            windows,
            fine_scale,
            own,
            halo,
            gain,
            jnp.asarray(PLACES.T.copy()),
            jnp.asarray(PLACES[:OWN].copy()),
            ones,
            fine_qkv,
            fine_out,
        ],
        (0, 1, 2),
        flops=2 * KEYS * depth * 3 * depth,
        nbytes=5 * 2**20,
    )
    bottom = call(
        merge_kernel,
        jax.ShapeDtypeStruct((NX, TOKENS, merge_w.shape[1]), BF16),
        [place, *gather_x(stream), merge_w],
        (0,),
        flops=2 * OWN * 4 * depth * merge_w.shape[1],
        nbytes=3 * 2**20,
    )
    bfull, query, pairs = call(
        project_kernel,
        (
            jax.ShapeDtypeStruct((OWN, deep), BF16),
            jax.ShapeDtypeStruct((OWN, 256), F32),
            jax.ShapeDtypeStruct((16, OWN, 2 * group), BF16),
        ),
        [place, *gather_x(bottom), ones, qkv_w],
        (0,),
        [pltpu.VMEM((OWN, deep), F32)],
        flops=2 * OWN * deep * 640,
        nbytes=4 * 2**20,
    )
    near = lax.all_to_all(pairs, ZY, 0, 0).reshape(16 * OWN, 2 * group)
    far = swap_core(near)
    batt = call(
        attend_kernel,
        jax.ShapeDtypeStruct((OWN, group), BF16),
        [bottom_scale, place, query, near, far],
        (0, 1),
        flops=2 * 3 * OWN * 3072 * 256 * 3,
        nbytes=3 * 2**20,
    )
    split = call(
        output_kernel,
        jax.ShapeDtypeStruct((NX, TOKENS, depth), BF16),
        [place, *gather_x(batt), bfull, bottom_out, split_w],
        (0,),
        flops=2 * OWN * deep * 2 * depth,
        nbytes=5 * 2**20,
    )
    upward = lax.all_to_all(split, "x", 0, 0)
    return call(
        mix_kernel,
        jax.ShapeDtypeStruct((height, width, depth), BF16),
        [stream, upward, skip_mix[None], jnp.asarray(own_to_grid(), BF16)],
        (),
        flops=2 * 128 * 96 * depth,
        nbytes=2**20,
    )


def solution(mesh):
    inner = Mesh(mesh.devices.reshape(4, 2, 2, 2, 4), ALL)
    placed = (
        P(GY, GX, None),
        P(),
        P(),
        P(),
        P(),
        P(),
        P(),
        P(),
        P(ALL, None),
        P(),
        P(),
        P(),
        P(None, ALL),
        P(),
    )
    return jax.shard_map(
        shards, mesh=inner, in_specs=placed, out_specs=P(GY, GX, None), check_vma=False
    )
```

```python
import math

import jax
import jax.numpy as jnp
import numpy as np
from jax import lax
from jax.experimental import pallas as pl
from jax.experimental.pallas import tpu as pltpu
from jax.sharding import Mesh, PartitionSpec as P

HEAD_DIM = 64
WIN = 7
REACH = WIN // 2
EPS = 1e-06
ROWS, COLS = 8, 12
OWN = ROWS * COLS
TOKENS = OWN // 4
KEYS = 256
FAR = 1000
BF16 = jnp.bfloat16
F32 = jnp.float32

ALL = ("z", "yl", "c", "yh", "x")
GY = ("z", "yl", "c")
GX = ("yh", "x")
REST = ("yl", "yh", "x")
NX = 4

VMEM_LIMIT = 40 * 2**20


def key_places():
    places = []
    for cols in (range(COLS), range(-REACH, 0), range(COLS, COLS + REACH)):
        places += [(r, c) for c in cols for r in range(ROWS)]
    for rows in (range(-REACH, 0), range(ROWS, ROWS + REACH)):
        places += [(r, c) for c in range(-REACH, COLS + REACH) for r in rows]
    places += [(FAR, FAR)] * (KEYS - len(places))
    return np.array(places, np.int32)


PLACES = key_places()


def reorder(flip):
    m = lax.broadcasted_iota(jnp.int32, (OWN, OWN), 1 if flip else 0)
    n = lax.broadcasted_iota(jnp.int32, (OWN, OWN), 0 if flip else 1)
    s = (m >= TOKENS).astype(jnp.int32) + (m >= 2 * TOKENS) + (m >= 3 * TOKENS)
    t = m - s * TOKENS
    source = (2 * (t // 4) + s % 2) * ROWS + 2 * (t % 4) + s // 2
    return (n == source).astype(F32).astype(BF16)


def block_ones():
    row = lax.broadcasted_iota(jnp.int32, (256, 256), 0) // HEAD_DIM
    col = lax.broadcasted_iota(jnp.int32, (256, 256), 1) // HEAD_DIM
    return (row == col).astype(F32).astype(BF16)


def dot(a, b):
    return jnp.dot(a, b, preferred_element_type=F32)


def dot_t(a, b):
    return lax.dot_general(a, b, (((1,), (1,)), ((), ())), preferred_element_type=F32)


def split_hi_lo(values):
    hi = values.astype(BF16)
    lo = (values - hi.astype(F32)).astype(BF16)
    return hi, lo


def unit_quad(values, ones):
    hi, lo = split_hi_lo(values * values)
    total = dot(hi, ones) + dot(lo, ones)
    return values * lax.rsqrt(total + EPS)


def full(shape):
    return pl.BlockSpec(memory_space=pltpu.VMEM)


def smem():
    return pl.BlockSpec(memory_space=pltpu.SMEM)


def call(body, out_shape, args, in_smem, scratch=(), flops=0, nbytes=0):
    return pl.pallas_call(
        body,
        out_shape=out_shape,
        in_specs=[smem() if i in in_smem else full(None) for i in range(len(args))],
        out_specs=jax.tree.map(lambda _: full(None), out_shape),
        scratch_shapes=list(scratch),
        compiler_params=pltpu.CompilerParams(vmem_limit_bytes=VMEM_LIMIT),
        cost_estimate=pl.CostEstimate(flops=flops, bytes_accessed=nbytes, transcendentals=0),
    )(*args)


def gain_kernel(step, row, freqs, gain):
    angles = step[0].astype(F32) * freqs[...]
    features = jnp.concatenate([jnp.cos(angles), jnp.sin(angles)], axis=1)
    gain[...] = 1.0 + 0.5 * (row[...].astype(F32) + features)


def fine_kernel(
    start, windows, scales, own, left, right, up, down, gain, key_place, query_place,
    qkv, out_w, stream, tokens,
):
    width = own.shape[2]
    tokens[KEYS - 8 :] = jnp.zeros((8, width), F32)
    tokens[:OWN] = own[...].astype(F32).reshape(OWN, width)
    at = OWN
    for strip in (left, right):
        tokens[at : at + REACH * ROWS] = strip[...].astype(F32).reshape(REACH * ROWS, width)
        at += REACH * ROWS
    for strip in (up, down):
        for c in range(strip.shape[0]):
            tokens[at : at + REACH] = strip[c].astype(F32)
            at += REACH
    x = tokens[...]
    mean = jnp.mean(x * x, axis=-1, keepdims=True)
    n_all = (x * lax.rsqrt(mean + EPS) * gain[...]).astype(BF16)
    n_own = n_all[:OWN]
    row_k, col_k = key_place[0:1, :], key_place[1:2, :]
    row_q, col_q = query_place[:, 0:1], query_place[:, 1:2]
    row_g, col_g = row_k + start[0], col_k + start[1]
    inside = (row_g >= 0) & (row_g < start[2]) & (col_g >= 0) & (col_g < start[3])
    apart = jnp.maximum(jnp.abs(row_k - row_q), jnp.abs(col_k - col_q))
    apart = jnp.where(inside, apart, FAR)

    ones = block_ones()
    lane = lax.broadcasted_iota(jnp.int32, (OWN, 256), 1) // HEAD_DIM
    update = x[:OWN]
    for quad in range(width // 256):
        at = quad * 256
        query = unit_quad(dot(n_own, qkv[:, at : at + 256]), ones)
        key = unit_quad(dot(n_all, qkv[:, width + at : width + at + 256]), ones).astype(BF16)
        value = dot(n_all, qkv[:, 2 * width + at : 2 * width + at + 256]).astype(BF16)
        hi, lo = split_hi_lo(query)
        rows = [jnp.where(lane == h, hi, 0) for h in range(4)]
        rows += [jnp.where(lane == h, lo, 0) for h in range(4)]
        score = dot_t(jnp.concatenate(rows, axis=0), key)
        score = score[: 4 * OWN] + score[4 * OWN :]
        weights, totals = [], []
        for h in range(4):
            head = quad * 4 + h
            radius = (windows[head] - 1) // 2
            part = scales[head] * score[h * OWN : (h + 1) * OWN]
            part = jnp.where(apart <= radius, part, -jnp.inf)
            part = jnp.exp(part - jnp.max(part, axis=-1, keepdims=True))
            totals.append(jnp.sum(part, axis=-1, keepdims=True))
            weights.append(part.astype(BF16))
        mixed = dot(jnp.concatenate(weights, axis=0), value)
        att = jnp.zeros((OWN, 256), F32)
        for h in range(4):
            att = jnp.where(lane == h, mixed[h * OWN : (h + 1) * OWN] / totals[h], att)
        update = update + dot(att.astype(BF16), out_w[at : at + 256, :])
    result = dot(reorder(False), update.astype(BF16))
    for s in range(4):
        stream[s] = result[s * TOKENS : (s + 1) * TOKENS].astype(BF16)


def merge_kernel(place, p0, p1, p2, p3, mine, other, bottom, weight):
    width = p0.shape[2]
    half = mine.shape[0] * mine.shape[1] // 8
    for i in range(8):
        for ref, core in ((mine, place[1]), (other, 1 - place[1])):
            at = pl.multiple_of(i * 2 * half + core * half, half)
            weight[pl.ds(at, half), :] = ref[i * 8 : i * 8 + 8].reshape(half, ref.shape[2])
    acc = None
    for s in range(4):
        rows = jnp.concatenate([p[s].astype(F32) for p in (p0, p1, p2, p3)], axis=0).astype(BF16)
        term = dot(rows, weight[s * width : (s + 1) * width, :])
        acc = term if acc is None else acc + term
    for k in range(NX):
        bottom[lax.rem(place[0] + NX - k, NX)] = acc[k * TOKENS : (k + 1) * TOKENS].astype(BF16)


def project_kernel(place, p0, p1, p2, p3, weight, bottom, query, pairs, whole):
    block = p0.shape[2]
    ones = block_ones()
    for k, p in enumerate((p0, p1, p2, p3)):
        at = pl.multiple_of(lax.rem(place[0] + NX - k, NX) * block, 128)
        rows = jnp.concatenate([p[i].astype(F32) for i in range(NX)], axis=0)
        whole[:, pl.ds(at, block)] = rows
    x = whole[...]
    bottom[...] = x.astype(BF16)
    mean = jnp.mean(x * x, axis=-1, keepdims=True)
    normed = (x * lax.rsqrt(mean + EPS)).astype(BF16)
    proj = dot(normed, weight[...])
    first = proj[:, :256]
    lane = lax.broadcasted_iota(jnp.int32, first.shape, 1)
    first = jnp.where(lane < 192, unit_quad(first, ones), first)
    kv = jnp.concatenate([first, proj[:, 256:384]], axis=1).astype(BF16)
    for i in range(pairs.shape[0]):
        pairs[i] = kv
    query[...] = unit_quad(proj[:, 384:640], ones)


def attend_part(scales, place, query, ref):
    lane = lax.broadcasted_iota(jnp.int32, query.shape, 1) // HEAD_DIM
    count = query.shape[0]
    hi, lo = split_hi_lo(query[...])
    rows = [jnp.where(lane == h, hi, 0) for h in range(3)]
    rows += [jnp.where(lane == h, lo, 0) for h in range(3)]
    scale = jnp.concatenate(
        [jnp.full((count, 1), scales[3 * place[0] + h], F32) for h in range(3)], axis=0
    )
    score = dot_t(jnp.concatenate(rows, axis=0), ref[:, :256])
    score = scale * (score[: 3 * count] + score[3 * count :])
    highest = jnp.max(score, axis=-1, keepdims=True)
    part = jnp.exp(score - highest)
    total = jnp.sum(part, axis=-1, keepdims=True)
    return highest, total, dot(part.astype(BF16), ref[:, 128:384])


def near_kernel(scales, place, query, near, highest, total, acc):
    highest[...], total[...], acc[...] = attend_part(scales, place, query, near)


def far_kernel(scales, place, query, far, near_highest, near_total, near_acc, out):
    count = query.shape[0]
    highest, total, acc = attend_part(scales, place, query, far)
    top = jnp.maximum(highest, near_highest[...])
    fade, near_fade = jnp.exp(highest - top), jnp.exp(near_highest[...] - top)
    acc = acc * fade + near_acc[...] * near_fade
    acc = acc / (total * fade + near_total[...] * near_fade)
    lane = lax.broadcasted_iota(jnp.int32, query.shape, 1) // HEAD_DIM
    att = jnp.zeros((count, 256), F32)
    for h in range(3):
        att = jnp.where(lane == h + 1, acc[h * count : (h + 1) * count], att)
    out[...] = att[:, 64:].astype(BF16)


def output_kernel(place, p0, p1, p2, p3, bottom, out_w, split_w, split):
    acc = bottom[...].astype(F32)
    block = p0.shape[1]
    for k, p in enumerate((p0, p1, p2, p3)):
        at = pl.multiple_of(lax.rem(place[0] + NX - k, NX) * block, 64)
        acc = acc + dot(p[...], out_w[pl.ds(at, block), :])
    result = dot_t(acc.astype(BF16), split_w[...])
    for i in range(NX):
        split[i] = result[i * TOKENS : (i + 1) * TOKENS].astype(BF16)


def mix_kernel(place, stream, u0, u1, u2, u3, mix, out, upward):
    for k, u in enumerate((u0, u1, u2, u3)):
        upward[lax.rem(place[0] + NX - k, NX)] = u[...].astype(F32)
    s = jnp.concatenate([stream[i].astype(F32) for i in range(4)], axis=0)
    u = upward[...].reshape(OWN, out.shape[2])
    mixed = (s + mix[...] * (u - s)).astype(BF16)
    grid = dot(reorder(True), mixed)
    out[...] = grid.reshape(out.shape).astype(BF16)


def shift(x, axis, size, step):
    return lax.ppermute(x, axis, [(i, i + step) for i in range(size) if 0 <= i + step < size])


def gather_z(x):
    return [x] + [
        lax.ppermute(x, "z", [(i, (i + s) % NX) for i in range(NX)]) for s in range(1, NX)
    ]


def scatter_z(x):
    z = lax.axis_index("z")
    parts = [lax.dynamic_index_in_dim(x, (z + s) % NX, 0, keepdims=False) for s in range(NX)]
    return parts[:1] + [
        lax.ppermute(parts[s], "z", [(i, (i + s) % NX) for i in range(NX)]) for s in range(1, NX)
    ]


def swap_core(x):
    return lax.ppermute(x, "c", [(0, 1), (1, 0)])


def after(x, *others):
    return lax.optimization_barrier((x, *others))[0]


def merge_columns(merge_weight):
    rows, width = merge_weight.shape
    block = width // NX
    parts = jnp.stack([merge_weight[:, i * block : (i + 1) * block] for i in range(NX)])
    parts = jnp.broadcast_to(parts[:, None], (NX, 16, rows, block)).reshape(16 * NX, rows, block)
    return lax.all_to_all(parts, ("z", *REST), 0, 0)


def spread(chunk):
    return jnp.broadcast_to(chunk[None], (16, *chunk.shape))


def split_columns(mine):
    rows, depth = mine.shape[1:]
    other = swap_core(mine)
    c = lax.axis_index("c")
    first = jnp.where(c == 0, mine, other).reshape(2, 8, rows, depth)
    second = jnp.where(c == 0, other, mine).reshape(2, 8, rows, depth)
    return jnp.stack([first, second], axis=1).reshape(32 * rows, depth)


def shards(
    fine,
    class_table,
    label,
    timestep,
    windows,
    fine_scale,
    fine_qkv,
    fine_out,
    merge_weight,
    bottom_scale,
    bottom_qkv,
    bottom_out,
    split_weight,
    skip_mix,
):
    height, width, depth = fine.shape
    own = fine.transpose(1, 0, 2)
    left = shift(own[width - REACH :], GX, 8, 1)
    right = shift(own[:REACH], GX, 8, -1)
    wide = jnp.concatenate([left, own, right], axis=0)
    up = shift(wide[:, height - REACH :], GY, 16, 1)
    down = shift(wide[:, :REACH], GY, 16, -1)
    row = lax.dynamic_slice_in_dim(class_table, label[0], 1, 0)
    half = depth // 2
    freqs = np.exp(np.float32(-math.log(10000.0)) * np.arange(half, dtype=np.float32) / half)
    gain = call(
        gain_kernel,
        jax.ShapeDtypeStruct((1, depth), F32),
        [timestep, row, jnp.asarray(freqs[None], F32)],
        (0,),
    )
    start = jnp.stack(
        [
            lax.axis_index(GY) * height,
            lax.axis_index(GX) * width,
            jnp.int32(16 * height),
            jnp.int32(8 * width),
        ]
    ).astype(jnp.int32)
    place = jnp.stack([lax.axis_index("z"), lax.axis_index("c")]).astype(jnp.int32)

    merge_w = merge_columns(merge_weight)
    stream = call(
        fine_kernel,
        jax.ShapeDtypeStruct((4, TOKENS, depth), BF16),
        [
            start, windows, fine_scale, own, left, right, up, down, gain,
            jnp.asarray(PLACES.T.copy()), jnp.asarray(PLACES[:OWN].copy()), fine_qkv, fine_out,
        ],
        (0, 1, 2),
        [pltpu.VMEM((KEYS, depth), F32)],
        flops=2 * KEYS * depth * 3 * depth,
        nbytes=5 * 2**20,
    )
    streams = gather_z(stream)
    split_w = lax.all_to_all(after(spread(split_weight.T), merge_w, up, down), REST, 0, 0)
    merge_w = after(merge_w, stream)
    block = merge_w.shape[2]
    bottom = call(
        merge_kernel,
        jax.ShapeDtypeStruct((NX, TOKENS, block), BF16),
        [place, *streams, merge_w, swap_core(merge_w)],
        (0,),
        [pltpu.VMEM((4 * depth, block), BF16)],
        flops=2 * OWN * 4 * depth * block,
        nbytes=3 * 2**20,
    )
    battn = bottom_out.shape[0]
    group = battn // NX
    deep = bottom_qkv.shape[0]
    weight = after(bottom_qkv, bottom)
    at = lax.axis_index("z") * group
    picked = [
        lax.dynamic_slice_in_dim(weight, part * battn + at, group, 1) for part in (1, 2, 0)
    ]
    qkv_w = jnp.concatenate(picked + [jnp.zeros((deep, 64), BF16)], axis=1)
    bfull, query, pairs = call(
        project_kernel,
        (
            jax.ShapeDtypeStruct((OWN, deep), BF16),
            jax.ShapeDtypeStruct((OWN, 256), F32),
            jax.ShapeDtypeStruct((16, OWN, 2 * group), BF16),
        ),
        [place, *gather_z(bottom), qkv_w],
        (0,),
        [pltpu.VMEM((OWN, deep), F32)],
        flops=2 * OWN * deep * 640,
        nbytes=4 * 2**20,
    )
    pairs = after(pairs, split_w)
    near = lax.all_to_all(pairs, REST, 0, 0).reshape(16 * OWN, 2 * group)
    far = swap_core(near)
    near_part = call(
        near_kernel,
        (
            jax.ShapeDtypeStruct((3 * OWN, 1), F32),
            jax.ShapeDtypeStruct((3 * OWN, 1), F32),
            jax.ShapeDtypeStruct((3 * OWN, 256), F32),
        ),
        [bottom_scale, place, query, near],
        (0, 1),
        flops=2 * 3 * OWN * 1536 * 256 * 3,
        nbytes=2 * 2**20,
    )
    batt = call(
        far_kernel,
        jax.ShapeDtypeStruct((OWN, group), BF16),
        [bottom_scale, place, query, far, *near_part],
        (0, 1),
        flops=2 * 3 * OWN * 1536 * 256 * 3,
        nbytes=2 * 2**20,
    )
    split_w = split_columns(after(split_w, batt))
    split = call(
        output_kernel,
        jax.ShapeDtypeStruct((NX, TOKENS, depth), BF16),
        [place, *gather_z(batt), bfull, bottom_out, split_w],
        (0,),
        flops=2 * OWN * deep * 2 * depth,
        nbytes=5 * 2**20,
    )
    mixed = call(
        mix_kernel,
        jax.ShapeDtypeStruct((width, height, depth), BF16),
        [place, stream, *scatter_z(split), skip_mix[None]],
        (0,),
        [pltpu.VMEM((4, TOKENS, depth), F32)],
        flops=2 * 128 * 96 * depth,
        nbytes=2**20,
    )
    return mixed.transpose(1, 0, 2)


def solution(mesh):
    inner = Mesh(mesh.devices.reshape(4, 2, 2, 2, 4), ALL)
    placed = (
        P(GY, GX, None),
        P(),
        P(),
        P(),
        P(),
        P(),
        P(),
        P(),
        P(ALL, None),
        P(),
        P(),
        P(),
        P(None, ALL),
        P(),
    )
    return jax.shard_map(
        shards, mesh=inner, in_specs=placed, out_specs=P(GY, GX, None), check_vma=False
    )
```

```python
import math

import jax
import jax.numpy as jnp
import numpy as np
from jax import lax
from jax.experimental import pallas as pl
from jax.experimental.pallas import tpu as pltpu
from jax.sharding import Mesh, PartitionSpec as P

HEAD_DIM = 64
WIN = 7
REACH = WIN // 2
EPS = 1e-06
ROWS, COLS = 8, 12
OWN = ROWS * COLS
TOKENS = OWN // 4
KEYS = 256
FAR = 1000
BF16 = jnp.bfloat16
F32 = jnp.float32

ALL = ("z", "yl", "c", "yh", "x")
GY = ("z", "yl", "c")
GX = ("yh", "x")
REST = ("yl", "yh", "x")
NX = 4

VMEM_LIMIT = 40 * 2**20


def key_places():
    places = []
    for cols in (range(COLS), range(-REACH, 0), range(COLS, COLS + REACH)):
        places += [(r, c) for c in cols for r in range(ROWS)]
    for rows in (range(-REACH, 0), range(ROWS, ROWS + REACH)):
        places += [(r, c) for c in range(-REACH, COLS + REACH) for r in rows]
    places += [(FAR, FAR)] * (KEYS - len(places))
    return np.array(places, np.int32)


PLACES = key_places()


def reorder(flip):
    m = lax.broadcasted_iota(jnp.int32, (OWN, OWN), 1 if flip else 0)
    n = lax.broadcasted_iota(jnp.int32, (OWN, OWN), 0 if flip else 1)
    s = (m >= TOKENS).astype(jnp.int32) + (m >= 2 * TOKENS) + (m >= 3 * TOKENS)
    t = m - s * TOKENS
    source = (2 * (t // 4) + s % 2) * ROWS + 2 * (t % 4) + s // 2
    return (n == source).astype(F32).astype(BF16)


def block_ones():
    row = lax.broadcasted_iota(jnp.int32, (256, 256), 0) // HEAD_DIM
    col = lax.broadcasted_iota(jnp.int32, (256, 256), 1) // HEAD_DIM
    return (row == col).astype(F32).astype(BF16)


def dot(a, b):
    return jnp.dot(a, b, preferred_element_type=F32)


def dot_t(a, b):
    return lax.dot_general(a, b, (((1,), (1,)), ((), ())), preferred_element_type=F32)


def split_hi_lo(values):
    hi = values.astype(BF16)
    lo = (values - hi.astype(F32)).astype(BF16)
    return hi, lo


def unit_quad(values, ones):
    hi, lo = split_hi_lo(values * values)
    total = dot(hi, ones) + dot(lo, ones)
    return values * lax.rsqrt(total + EPS)


def full(shape):
    return pl.BlockSpec(memory_space=pltpu.VMEM)


def smem():
    return pl.BlockSpec(memory_space=pltpu.SMEM)


def call(body, out_shape, args, in_smem, scratch=(), flops=0, nbytes=0):
    return pl.pallas_call(
        body,
        out_shape=out_shape,
        in_specs=[smem() if i in in_smem else full(None) for i in range(len(args))],
        out_specs=jax.tree.map(lambda _: full(None), out_shape),
        scratch_shapes=list(scratch),
        compiler_params=pltpu.CompilerParams(vmem_limit_bytes=VMEM_LIMIT),
        cost_estimate=pl.CostEstimate(flops=flops, bytes_accessed=nbytes, transcendentals=0),
    )(*args)


def gain_kernel(step, row, freqs, gain):
    angles = step[0].astype(F32) * freqs[...]
    features = jnp.concatenate([jnp.cos(angles), jnp.sin(angles)], axis=1)
    gain[...] = 1.0 + 0.5 * (row[...].astype(F32) + features)


def normalise(x, gain):
    mean = jnp.mean(x * x, axis=-1, keepdims=True)
    return (x * lax.rsqrt(mean + EPS) * gain).astype(BF16)


def own_kernel(own, gain, qkv, out_w, query, key, value):
    width = own.shape[2]
    ones = block_ones()
    tokens = normalise(own[...].astype(F32).reshape(OWN, width), gain[...])
    for at in range(0, width, 256):
        here = slice(at, at + 256)
        query[:, here] = unit_quad(dot(tokens, qkv[:, here]), ones)
        part = dot(tokens, qkv[:, width + at : width + at + 256])
        key[:, here] = unit_quad(part, ones).astype(BF16)
        value[:, here] = dot(tokens, qkv[:, 2 * width + at : 2 * width + at + 256]).astype(BF16)


def fine_kernel(
    start, windows, scales, own, left, right, up, down, gain, key_place, query_place,
    own_query, own_key, own_value, qkv, out_w, stream, tokens,
):
    width = own.shape[2]
    tokens[KEYS - OWN - 8 :] = jnp.zeros((8, width), F32)
    at = 0
    for strip in (left, right):
        tokens[at : at + REACH * ROWS] = strip[...].astype(F32).reshape(REACH * ROWS, width)
        at += REACH * ROWS
    for strip in (up, down):
        for c in range(strip.shape[0]):
            tokens[at : at + REACH] = strip[c].astype(F32)
            at += REACH
    halo = normalise(tokens[...], gain[...])
    row_k, col_k = key_place[0:1, :], key_place[1:2, :]
    row_q, col_q = query_place[:, 0:1], query_place[:, 1:2]
    row_g, col_g = row_k + start[0], col_k + start[1]
    inside = (row_g >= 0) & (row_g < start[2]) & (col_g >= 0) & (col_g < start[3])
    apart = jnp.maximum(jnp.abs(row_k - row_q), jnp.abs(col_k - col_q))
    apart = jnp.where(inside, apart, FAR)

    ones = block_ones()
    lane = lax.broadcasted_iota(jnp.int32, (OWN, 256), 1) // HEAD_DIM
    update = own[...].astype(F32).reshape(OWN, width)
    for quad in range(width // 256):
        at = quad * 256
        query = own_query[:, at : at + 256]
        key = unit_quad(dot(halo, qkv[:, width + at : width + at + 256]), ones).astype(BF16)
        key = jnp.concatenate([own_key[:, at : at + 256], key], axis=0)
        value = dot(halo, qkv[:, 2 * width + at : 2 * width + at + 256]).astype(BF16)
        value = jnp.concatenate([own_value[:, at : at + 256], value], axis=0)
        hi, lo = split_hi_lo(query)
        rows = [jnp.where(lane == h, hi, 0) for h in range(4)]
        rows += [jnp.where(lane == h, lo, 0) for h in range(4)]
        score = dot_t(jnp.concatenate(rows, axis=0), key)
        score = score[: 4 * OWN] + score[4 * OWN :]
        weights, totals = [], []
        for h in range(4):
            head = quad * 4 + h
            radius = (windows[head] - 1) // 2
            part = scales[head] * score[h * OWN : (h + 1) * OWN]
            part = jnp.where(apart <= radius, part, -jnp.inf)
            part = jnp.exp(part - jnp.max(part, axis=-1, keepdims=True))
            totals.append(jnp.sum(part, axis=-1, keepdims=True))
            weights.append(part.astype(BF16))
        mixed = dot(jnp.concatenate(weights, axis=0), value)
        att = jnp.zeros((OWN, 256), F32)
        for h in range(4):
            att = jnp.where(lane == h, mixed[h * OWN : (h + 1) * OWN] / totals[h], att)
        update = update + dot(att.astype(BF16), out_w[at : at + 256, :])
    result = dot(reorder(False), update.astype(BF16))
    for s in range(4):
        stream[s] = result[s * TOKENS : (s + 1) * TOKENS].astype(BF16)


def merge_kernel(place, p0, p1, p2, p3, mine, other, bottom, weight):
    width = p0.shape[2]
    half = mine.shape[0] * mine.shape[1] // 8
    for i in range(8):
        for ref, core in ((mine, place[1]), (other, 1 - place[1])):
            at = pl.multiple_of(i * 2 * half + core * half, half)
            weight[pl.ds(at, half), :] = ref[i * 8 : i * 8 + 8].reshape(half, ref.shape[2])
    acc = None
    for s in range(4):
        rows = jnp.concatenate([p[s].astype(F32) for p in (p0, p1, p2, p3)], axis=0).astype(BF16)
        term = dot(rows, weight[s * width : (s + 1) * width, :])
        acc = term if acc is None else acc + term
    for k in range(NX):
        bottom[lax.rem(place[0] + NX - k, NX)] = acc[k * TOKENS : (k + 1) * TOKENS].astype(BF16)


def project_kernel(place, p0, p1, p2, p3, weight, bottom, query, pairs, whole):
    block = p0.shape[2]
    ones = block_ones()
    for k, p in enumerate((p0, p1, p2, p3)):
        at = pl.multiple_of(lax.rem(place[0] + NX - k, NX) * block, 128)
        rows = jnp.concatenate([p[i].astype(F32) for i in range(NX)], axis=0)
        whole[:, pl.ds(at, block)] = rows
    x = whole[...]
    bottom[...] = x.astype(BF16)
    mean = jnp.mean(x * x, axis=-1, keepdims=True)
    normed = (x * lax.rsqrt(mean + EPS)).astype(BF16)
    proj = dot(normed, weight[...])
    first = proj[:, :256]
    lane = lax.broadcasted_iota(jnp.int32, first.shape, 1)
    first = jnp.where(lane < 192, unit_quad(first, ones), first)
    kv = jnp.concatenate([first, proj[:, 256:384]], axis=1).astype(BF16)
    for i in range(pairs.shape[0]):
        pairs[i] = kv
    query[...] = unit_quad(proj[:, 384:640], ones)


def attend_part(scales, place, query, ref):
    lane = lax.broadcasted_iota(jnp.int32, query.shape, 1) // HEAD_DIM
    count = query.shape[0]
    hi, lo = split_hi_lo(query[...])
    rows = [jnp.where(lane == h, hi, 0) for h in range(3)]
    rows += [jnp.where(lane == h, lo, 0) for h in range(3)]
    scale = jnp.concatenate(
        [jnp.full((count, 1), scales[3 * place[0] + h], F32) for h in range(3)], axis=0
    )
    score = dot_t(jnp.concatenate(rows, axis=0), ref[:, :256])
    score = scale * (score[: 3 * count] + score[3 * count :])
    highest = jnp.max(score, axis=-1, keepdims=True)
    part = jnp.exp(score - highest)
    total = jnp.sum(part, axis=-1, keepdims=True)
    return highest, total, dot(part.astype(BF16), ref[:, 128:384])


def near_kernel(scales, place, query, near, highest, total, acc):
    highest[...], total[...], acc[...] = attend_part(scales, place, query, near)


def far_kernel(scales, place, query, far, near_highest, near_total, near_acc, out):
    count = query.shape[0]
    highest, total, acc = attend_part(scales, place, query, far)
    top = jnp.maximum(highest, near_highest[...])
    fade, near_fade = jnp.exp(highest - top), jnp.exp(near_highest[...] - top)
    acc = acc * fade + near_acc[...] * near_fade
    acc = acc / (total * fade + near_total[...] * near_fade)
    lane = lax.broadcasted_iota(jnp.int32, query.shape, 1) // HEAD_DIM
    att = jnp.zeros((count, 256), F32)
    for h in range(3):
        att = jnp.where(lane == h + 1, acc[h * count : (h + 1) * count], att)
    out[...] = att[:, 64:].astype(BF16)


def output_kernel(place, p0, p1, p2, p3, bottom, out_w, split_w, split):
    acc = bottom[...].astype(F32)
    block = p0.shape[1]
    for k, p in enumerate((p0, p1, p2, p3)):
        at = pl.multiple_of(lax.rem(place[0] + NX - k, NX) * block, 64)
        acc = acc + dot(p[...], out_w[pl.ds(at, block), :])
    result = dot_t(acc.astype(BF16), split_w[...])
    for i in range(NX):
        split[i] = result[i * TOKENS : (i + 1) * TOKENS].astype(BF16)


def mix_kernel(place, stream, u0, u1, u2, u3, mix, out, upward):
    for k, u in enumerate((u0, u1, u2, u3)):
        upward[lax.rem(place[0] + NX - k, NX)] = u[...].astype(F32)
    s = jnp.concatenate([stream[i].astype(F32) for i in range(4)], axis=0)
    u = upward[...].reshape(OWN, out.shape[2])
    mixed = (s + mix[...] * (u - s)).astype(BF16)
    grid = dot(reorder(True), mixed)
    out[...] = grid.reshape(out.shape).astype(BF16)


def shift(x, axis, size, step):
    return lax.ppermute(x, axis, [(i, i + step) for i in range(size) if 0 <= i + step < size])


def gather_z(x):
    return [x] + [
        lax.ppermute(x, "z", [(i, (i + s) % NX) for i in range(NX)]) for s in range(1, NX)
    ]


def scatter_z(x):
    z = lax.axis_index("z")
    parts = [lax.dynamic_index_in_dim(x, (z + s) % NX, 0, keepdims=False) for s in range(NX)]
    return parts[:1] + [
        lax.ppermute(parts[s], "z", [(i, (i + s) % NX) for i in range(NX)]) for s in range(1, NX)
    ]


def swap_core(x):
    return lax.ppermute(x, "c", [(0, 1), (1, 0)])


def after(x, *others):
    return lax.optimization_barrier((x, *others))[0]


def merge_columns(merge_weight):
    rows, width = merge_weight.shape
    block = width // NX
    parts = jnp.stack([merge_weight[:, i * block : (i + 1) * block] for i in range(NX)])
    parts = jnp.broadcast_to(parts[:, None], (NX, 16, rows, block)).reshape(16 * NX, rows, block)
    return lax.all_to_all(parts, ("z", *REST), 0, 0)


def spread(chunk):
    return jnp.broadcast_to(chunk[None], (16, *chunk.shape))


def split_columns(mine):
    rows, depth = mine.shape[1:]
    other = swap_core(mine)
    c = lax.axis_index("c")
    first = jnp.where(c == 0, mine, other).reshape(2, 8, rows, depth)
    second = jnp.where(c == 0, other, mine).reshape(2, 8, rows, depth)
    return jnp.stack([first, second], axis=1).reshape(32 * rows, depth)


def shards(
    fine,
    class_table,
    label,
    timestep,
    windows,
    fine_scale,
    fine_qkv,
    fine_out,
    merge_weight,
    bottom_scale,
    bottom_qkv,
    bottom_out,
    split_weight,
    skip_mix,
):
    height, width, depth = fine.shape
    own = fine.transpose(1, 0, 2)
    left = shift(own[width - REACH :], GX, 8, 1)
    right = shift(own[:REACH], GX, 8, -1)
    wide = jnp.concatenate([left, own, right], axis=0)
    row = lax.dynamic_slice_in_dim(class_table, label[0], 1, 0)
    half = depth // 2
    freqs = np.exp(np.float32(-math.log(10000.0)) * np.arange(half, dtype=np.float32) / half)
    gain = call(
        gain_kernel,
        jax.ShapeDtypeStruct((1, depth), F32),
        [timestep, row, jnp.asarray(freqs[None], F32)],
        (0,),
    )
    own_heads = call(
        own_kernel,
        (
            jax.ShapeDtypeStruct((OWN, depth), F32),
            jax.ShapeDtypeStruct((OWN, depth), BF16),
            jax.ShapeDtypeStruct((OWN, depth), BF16),
        ),
        [own, gain, fine_qkv, fine_out],
        (),
        flops=2 * OWN * depth * 3 * depth,
        nbytes=5 * 2**20,
    )
    chunks = spread(split_weight.T)
    wide = after(wide, chunks, *own_heads)
    up = shift(wide[:, height - REACH :], GY, 16, 1)
    down = shift(wide[:, :REACH], GY, 16, -1)
    start = jnp.stack(
        [
            lax.axis_index(GY) * height,
            lax.axis_index(GX) * width,
            jnp.int32(16 * height),
            jnp.int32(8 * width),
        ]
    ).astype(jnp.int32)
    place = jnp.stack([lax.axis_index("z"), lax.axis_index("c")]).astype(jnp.int32)

    merge_w = merge_columns(merge_weight)
    stream = call(
        fine_kernel,
        jax.ShapeDtypeStruct((4, TOKENS, depth), BF16),
        [
            start, windows, fine_scale, own, left, right, up, down, gain,
            jnp.asarray(PLACES.T.copy()), jnp.asarray(PLACES[:OWN].copy()), *own_heads, fine_qkv, fine_out,
        ],
        (0, 1, 2),
        [pltpu.VMEM((KEYS - OWN, depth), F32)],
        flops=2 * KEYS * depth * 3 * depth,
        nbytes=5 * 2**20,
    )
    streams = gather_z(stream)
    split_w = lax.all_to_all(after(chunks, merge_w, up, down), REST, 0, 0)
    merge_w = after(merge_w, stream)
    block = merge_w.shape[2]
    bottom = call(
        merge_kernel,
        jax.ShapeDtypeStruct((NX, TOKENS, block), BF16),
        [place, *streams, merge_w, swap_core(merge_w)],
        (0,),
        [pltpu.VMEM((4 * depth, block), BF16)],
        flops=2 * OWN * 4 * depth * block,
        nbytes=3 * 2**20,
    )
    battn = bottom_out.shape[0]
    group = battn // NX
    deep = bottom_qkv.shape[0]
    weight = after(bottom_qkv, bottom)
    at = lax.axis_index("z") * group
    picked = [
        lax.dynamic_slice_in_dim(weight, part * battn + at, group, 1) for part in (1, 2, 0)
    ]
    qkv_w = jnp.concatenate(picked + [jnp.zeros((deep, 64), BF16)], axis=1)
    bfull, query, pairs = call(
        project_kernel,
        (
            jax.ShapeDtypeStruct((OWN, deep), BF16),
            jax.ShapeDtypeStruct((OWN, 256), F32),
            jax.ShapeDtypeStruct((16, OWN, 2 * group), BF16),
        ),
        [place, *gather_z(bottom), qkv_w],
        (0,),
        [pltpu.VMEM((OWN, deep), F32)],
        flops=2 * OWN * deep * 640,
        nbytes=4 * 2**20,
    )
    pairs = after(pairs, split_w)
    near = lax.all_to_all(pairs, REST, 0, 0).reshape(16 * OWN, 2 * group)
    far = swap_core(near)
    near_part = call(
        near_kernel,
        (
            jax.ShapeDtypeStruct((3 * OWN, 1), F32),
            jax.ShapeDtypeStruct((3 * OWN, 1), F32),
            jax.ShapeDtypeStruct((3 * OWN, 256), F32),
        ),
        [bottom_scale, place, query, near],
        (0, 1),
        flops=2 * 3 * OWN * 1536 * 256 * 3,
        nbytes=2 * 2**20,
    )
    batt = call(
        far_kernel,
        jax.ShapeDtypeStruct((OWN, group), BF16),
        [bottom_scale, place, query, far, *near_part],
        (0, 1),
        flops=2 * 3 * OWN * 1536 * 256 * 3,
        nbytes=2 * 2**20,
    )
    split_w = split_columns(after(split_w, batt))
    split = call(
        output_kernel,
        jax.ShapeDtypeStruct((NX, TOKENS, depth), BF16),
        [place, *gather_z(batt), bfull, bottom_out, split_w],
        (0,),
        flops=2 * OWN * deep * 2 * depth,
        nbytes=5 * 2**20,
    )
    mixed = call(
        mix_kernel,
        jax.ShapeDtypeStruct((width, height, depth), BF16),
        [place, stream, *scatter_z(split), skip_mix[None]],
        (0,),
        [pltpu.VMEM((4, TOKENS, depth), F32)],
        flops=2 * 128 * 96 * depth,
        nbytes=2**20,
    )
    return mixed.transpose(1, 0, 2)


def solution(mesh):
    inner = Mesh(mesh.devices.reshape(4, 2, 2, 2, 4), ALL)
    placed = (
        P(GY, GX, None),
        P(),
        P(),
        P(),
        P(),
        P(),
        P(),
        P(),
        P(ALL, None),
        P(),
        P(),
        P(),
        P(None, ALL),
        P(),
    )
    return jax.shard_map(
        shards, mesh=inner, in_specs=placed, out_specs=P(GY, GX, None), check_vma=False
    )
```

```python
import math

import jax
import jax.numpy as jnp
import numpy as np
from jax import lax
from jax.experimental import pallas as pl
from jax.experimental.pallas import tpu as pltpu
from jax.sharding import Mesh, PartitionSpec as P

HEAD_DIM = 64
WIN = 7
REACH = WIN // 2
EPS = 1e-06
ROWS, COLS = 8, 12
OWN = ROWS * COLS
TOKENS = OWN // 4
KEYS = 256
FAR = 1000
BF16 = jnp.bfloat16
F32 = jnp.float32

ALL = ("z", "yl", "c", "yh", "x")
GY = ("z", "yl", "c")
GX = ("yh", "x")
REST = ("yl", "yh", "x")
NX = 4

VMEM_LIMIT = 40 * 2**20


def key_places():
    places = []
    for cols in (range(COLS), range(-REACH, 0), range(COLS, COLS + REACH)):
        places += [(r, c) for c in cols for r in range(ROWS)]
    for rows in (range(-REACH, 0), range(ROWS, ROWS + REACH)):
        places += [(r, c) for c in range(-REACH, COLS + REACH) for r in rows]
    places += [(FAR, FAR)] * (KEYS - len(places))
    return np.array(places, np.int32)


PLACES = key_places()


def reorder(flip):
    m = lax.broadcasted_iota(jnp.int32, (OWN, OWN), 1 if flip else 0)
    n = lax.broadcasted_iota(jnp.int32, (OWN, OWN), 0 if flip else 1)
    s = (m >= TOKENS).astype(jnp.int32) + (m >= 2 * TOKENS) + (m >= 3 * TOKENS)
    t = m - s * TOKENS
    source = (2 * (t // 4) + s % 2) * ROWS + 2 * (t % 4) + s // 2
    return (n == source).astype(F32).astype(BF16)


def block_ones():
    row = lax.broadcasted_iota(jnp.int32, (256, 256), 0) // HEAD_DIM
    col = lax.broadcasted_iota(jnp.int32, (256, 256), 1) // HEAD_DIM
    return (row == col).astype(F32).astype(BF16)


def dot(a, b):
    return jnp.dot(a, b, preferred_element_type=F32)


def dot_t(a, b):
    return lax.dot_general(a, b, (((1,), (1,)), ((), ())), preferred_element_type=F32)


def split_hi_lo(values):
    hi = values.astype(BF16)
    lo = (values - hi.astype(F32)).astype(BF16)
    return hi, lo


def unit_quad(values, ones):
    hi, lo = split_hi_lo(values * values)
    total = dot(hi, ones) + dot(lo, ones)
    return values * lax.rsqrt(total + EPS)


def full(shape):
    return pl.BlockSpec(memory_space=pltpu.VMEM)


def smem():
    return pl.BlockSpec(memory_space=pltpu.SMEM)


def call(body, out_shape, args, in_smem, scratch=(), flops=0, nbytes=0):
    return pl.pallas_call(
        body,
        out_shape=out_shape,
        in_specs=[smem() if i in in_smem else full(None) for i in range(len(args))],
        out_specs=jax.tree.map(lambda _: full(None), out_shape),
        scratch_shapes=list(scratch),
        compiler_params=pltpu.CompilerParams(vmem_limit_bytes=VMEM_LIMIT),
        cost_estimate=pl.CostEstimate(flops=flops, bytes_accessed=nbytes, transcendentals=0),
    )(*args)


def gain_kernel(step, row, freqs, gain):
    angles = step[0].astype(F32) * freqs[...]
    features = jnp.concatenate([jnp.cos(angles), jnp.sin(angles)], axis=1)
    gain[...] = 1.0 + 0.5 * (row[...].astype(F32) + features)


def normalise(x, gain):
    mean = jnp.mean(x * x, axis=-1, keepdims=True)
    return (x * lax.rsqrt(mean + EPS) * gain).astype(BF16)


def own_kernel(own, gain, qkv, out_w, query, key, value):
    width = own.shape[2]
    ones = block_ones()
    tokens = normalise(own[...].astype(F32).reshape(OWN, width), gain[...])
    for at in range(0, width, 256):
        here = slice(at, at + 256)
        query[:, here] = unit_quad(dot(tokens, qkv[:, here]), ones)
        part = dot(tokens, qkv[:, width + at : width + at + 256])
        key[:, here] = unit_quad(part, ones).astype(BF16)
        value[:, here] = dot(tokens, qkv[:, 2 * width + at : 2 * width + at + 256]).astype(BF16)


def fine_kernel(
    start, windows, scales, own, left, right, up, down, gain, key_place, query_place,
    own_query, own_key, own_value, qkv, out_w, stream, tokens,
):
    width = own.shape[2]
    tokens[KEYS - OWN - 8 :] = jnp.zeros((8, width), F32)
    at = 0
    for strip in (left, right):
        tokens[at : at + REACH * ROWS] = strip[...].astype(F32).reshape(REACH * ROWS, width)
        at += REACH * ROWS
    for strip in (up, down):
        for c in range(strip.shape[0]):
            tokens[at : at + REACH] = strip[c].astype(F32)
            at += REACH
    halo = normalise(tokens[...], gain[...])
    row_k, col_k = key_place[0:1, :], key_place[1:2, :]
    row_q, col_q = query_place[:, 0:1], query_place[:, 1:2]
    row_g, col_g = row_k + start[0], col_k + start[1]
    inside = (row_g >= 0) & (row_g < start[2]) & (col_g >= 0) & (col_g < start[3])
    apart = jnp.maximum(jnp.abs(row_k - row_q), jnp.abs(col_k - col_q))
    apart = jnp.where(inside, apart, FAR)

    ones = block_ones()
    lane = lax.broadcasted_iota(jnp.int32, (OWN, 256), 1) // HEAD_DIM
    update = own[...].astype(F32).reshape(OWN, width)
    for quad in range(width // 256):
        at = quad * 256
        query = own_query[:, at : at + 256]
        key = unit_quad(dot(halo, qkv[:, width + at : width + at + 256]), ones).astype(BF16)
        key = jnp.concatenate([own_key[:, at : at + 256], key], axis=0)
        value = dot(halo, qkv[:, 2 * width + at : 2 * width + at + 256]).astype(BF16)
        value = jnp.concatenate([own_value[:, at : at + 256], value], axis=0)
        hi, lo = split_hi_lo(query)
        rows = [jnp.where(lane == h, hi, 0) for h in range(4)]
        rows += [jnp.where(lane == h, lo, 0) for h in range(4)]
        score = dot_t(jnp.concatenate(rows, axis=0), key)
        score = score[: 4 * OWN] + score[4 * OWN :]
        weights, totals = [], []
        for h in range(4):
            head = quad * 4 + h
            radius = (windows[head] - 1) // 2
            part = scales[head] * score[h * OWN : (h + 1) * OWN]
            part = jnp.where(apart <= radius, part, -jnp.inf)
            part = jnp.exp(part - jnp.max(part, axis=-1, keepdims=True))
            totals.append(jnp.sum(part, axis=-1, keepdims=True))
            weights.append(part.astype(BF16))
        mixed = dot(jnp.concatenate(weights, axis=0), value)
        att = jnp.zeros((OWN, 256), F32)
        for h in range(4):
            att = jnp.where(lane == h, mixed[h * OWN : (h + 1) * OWN] / totals[h], att)
        update = update + dot(att.astype(BF16), out_w[at : at + 256, :])
    result = dot(reorder(False), update.astype(BF16))
    for s in range(4):
        stream[s] = result[s * TOKENS : (s + 1) * TOKENS].astype(BF16)


def merge_kernel(place, p0, p1, p2, p3, mine, other, bottom, weight):
    width = p0.shape[2]
    half = mine.shape[0] * mine.shape[1] // 8
    for i in range(8):
        for ref, core in ((mine, place[1]), (other, 1 - place[1])):
            at = pl.multiple_of(i * 2 * half + core * half, half)
            weight[pl.ds(at, half), :] = ref[i * 8 : i * 8 + 8].reshape(half, ref.shape[2])
    acc = None
    for s in range(4):
        rows = jnp.concatenate([p[s].astype(F32) for p in (p0, p1, p2, p3)], axis=0).astype(BF16)
        term = dot(rows, weight[s * width : (s + 1) * width, :])
        acc = term if acc is None else acc + term
    for k in range(NX):
        bottom[lax.rem(place[0] + NX - k, NX)] = acc[k * TOKENS : (k + 1) * TOKENS].astype(BF16)


def project_kernel(place, p0, p1, p2, p3, weight, bottom, query, pairs, whole):
    block = p0.shape[2]
    ones = block_ones()
    for k, p in enumerate((p0, p1, p2, p3)):
        at = pl.multiple_of(lax.rem(place[0] + NX - k, NX) * block, 128)
        rows = jnp.concatenate([p[i].astype(F32) for i in range(NX)], axis=0)
        whole[:, pl.ds(at, block)] = rows
    x = whole[...]
    bottom[...] = x.astype(BF16)
    mean = jnp.mean(x * x, axis=-1, keepdims=True)
    normed = (x * lax.rsqrt(mean + EPS)).astype(BF16)
    proj = dot(normed, weight[...])
    first = proj[:, :256]
    lane = lax.broadcasted_iota(jnp.int32, first.shape, 1)
    first = jnp.where(lane < 192, unit_quad(first, ones), first)
    kv = jnp.concatenate([first, proj[:, 256:384]], axis=1).astype(BF16)
    for i in range(pairs.shape[0]):
        pairs[i] = kv
    query[...] = unit_quad(proj[:, 384:640], ones)


def attend_part(scales, place, query, ref):
    lane = lax.broadcasted_iota(jnp.int32, query.shape, 1) // HEAD_DIM
    count = query.shape[0]
    hi, lo = split_hi_lo(query[...])
    rows = [jnp.where(lane == h, hi, 0) for h in range(3)]
    rows += [jnp.where(lane == h, lo, 0) for h in range(3)]
    scale = jnp.concatenate(
        [jnp.full((count, 1), scales[3 * place[0] + h], F32) for h in range(3)], axis=0
    )
    score = dot_t(jnp.concatenate(rows, axis=0), ref[:, :256])
    score = scale * (score[: 3 * count] + score[3 * count :])
    highest = jnp.max(score, axis=-1, keepdims=True)
    part = jnp.exp(score - highest)
    total = jnp.sum(part, axis=-1, keepdims=True)
    return highest, total, dot(part.astype(BF16), ref[:, 128:384])


def near_kernel(scales, place, query, near, highest, total, acc):
    highest[...], total[...], acc[...] = attend_part(scales, place, query, near)


def far_kernel(scales, place, query, far, near_highest, near_total, near_acc, out):
    count = query.shape[0]
    highest, total, acc = attend_part(scales, place, query, far)
    top = jnp.maximum(highest, near_highest[...])
    fade, near_fade = jnp.exp(highest - top), jnp.exp(near_highest[...] - top)
    acc = acc * fade + near_acc[...] * near_fade
    acc = acc / (total * fade + near_total[...] * near_fade)
    lane = lax.broadcasted_iota(jnp.int32, query.shape, 1) // HEAD_DIM
    att = jnp.zeros((count, 256), F32)
    for h in range(3):
        att = jnp.where(lane == h + 1, acc[h * count : (h + 1) * count], att)
    out[...] = att[:, 64:].astype(BF16)


def arrange_kernel(place, mine, other, weight):
    for ref, core in ((mine, place[1]), (other, 1 - place[1])):
        for step in range(4):
            yl = place[2] if step < 2 else 1 - place[2]
            yh = place[3] if step % 2 == 0 else 1 - place[3]
            for k in range(4):
                x = lax.rem(place[4] + 4 - k, 4)
                weight[(yl * 2 + core) * 8 + yh * 4 + x] = ref[step, k]


def output_kernel(place, p0, p1, p2, p3, bottom, out_w, split_w, split):
    acc = bottom[...].astype(F32)
    block = p0.shape[1]
    for k, p in enumerate((p0, p1, p2, p3)):
        at = pl.multiple_of(lax.rem(place[0] + NX - k, NX) * block, 64)
        acc = acc + dot(p[...], out_w[pl.ds(at, block), :])
    result = dot_t(acc.astype(BF16), split_w[...])
    for i in range(NX):
        split[i] = result[i * TOKENS : (i + 1) * TOKENS].astype(BF16)


def mix_kernel(place, stream, u0, u1, u2, u3, mix, out, upward):
    for k, u in enumerate((u0, u1, u2, u3)):
        upward[lax.rem(place[0] + NX - k, NX)] = u[...].astype(F32)
    s = jnp.concatenate([stream[i].astype(F32) for i in range(4)], axis=0)
    u = upward[...].reshape(OWN, out.shape[2])
    mixed = (s + mix[...] * (u - s)).astype(BF16)
    grid = dot(reorder(True), mixed)
    out[...] = grid.reshape(out.shape).astype(BF16)


def shift(x, axis, size, step):
    return lax.ppermute(x, axis, [(i, i + step) for i in range(size) if 0 <= i + step < size])


def gather_z(x):
    return [x] + [
        lax.ppermute(x, "z", [(i, (i + s) % NX) for i in range(NX)]) for s in range(1, NX)
    ]


def scatter_z(x):
    z = lax.axis_index("z")
    parts = [lax.dynamic_index_in_dim(x, (z + s) % NX, 0, keepdims=False) for s in range(NX)]
    return parts[:1] + [
        lax.ppermute(parts[s], "z", [(i, (i + s) % NX) for i in range(NX)]) for s in range(1, NX)
    ]


def swap_core(x):
    return lax.ppermute(x, "c", [(0, 1), (1, 0)])


def after(x, *others):
    return lax.optimization_barrier((x, *others))[0]


def merge_columns(merge_weight):
    rows, width = merge_weight.shape
    block = width // NX
    parts = jnp.stack([merge_weight[:, i * block : (i + 1) * block] for i in range(NX)])
    parts = jnp.broadcast_to(parts[:, None], (NX, 16, rows, block)).reshape(16 * NX, rows, block)
    return lax.all_to_all(parts, ("z", *REST), 0, 0)


def gather_x(x):
    return jnp.stack(
        [x] + [lax.ppermute(x, "x", [(i, (i + s) % 4) for i in range(4)]) for s in range(1, 4)]
    )


def gather_y(x):
    return [x] + [
        lax.ppermute(x, ("yl", "yh"), [(i, i ^ s) for i in range(4)]) for s in range(1, 4)
    ]


def shards(
    fine,
    class_table,
    label,
    timestep,
    windows,
    fine_scale,
    fine_qkv,
    fine_out,
    merge_weight,
    bottom_scale,
    bottom_qkv,
    bottom_out,
    split_weight,
    skip_mix,
):
    height, width, depth = fine.shape
    own = fine.transpose(1, 0, 2)
    left = shift(own[width - REACH :], GX, 8, 1)
    right = shift(own[:REACH], GX, 8, -1)
    wide = jnp.concatenate([left, own, right], axis=0)
    row = lax.dynamic_slice_in_dim(class_table, label[0], 1, 0)
    half = depth // 2
    freqs = np.exp(np.float32(-math.log(10000.0)) * np.arange(half, dtype=np.float32) / half)
    gain = call(
        gain_kernel,
        jax.ShapeDtypeStruct((1, depth), F32),
        [timestep, row, jnp.asarray(freqs[None], F32)],
        (0,),
    )
    own_heads = call(
        own_kernel,
        (
            jax.ShapeDtypeStruct((OWN, depth), F32),
            jax.ShapeDtypeStruct((OWN, depth), BF16),
            jax.ShapeDtypeStruct((OWN, depth), BF16),
        ),
        [own, gain, fine_qkv, fine_out],
        (),
        flops=2 * OWN * depth * 3 * depth,
        nbytes=5 * 2**20,
    )
    chunk = split_weight.T
    wide = after(wide, chunk, *own_heads)
    up = shift(wide[:, height - REACH :], GY, 16, 1)
    down = shift(wide[:, :REACH], GY, 16, -1)
    start = jnp.stack(
        [
            lax.axis_index(GY) * height,
            lax.axis_index(GX) * width,
            jnp.int32(16 * height),
            jnp.int32(8 * width),
        ]
    ).astype(jnp.int32)
    place = jnp.stack([lax.axis_index(name) for name in ("z", "c", "yl", "yh", "x")])
    place = place.astype(jnp.int32)

    merge_w = merge_columns(merge_weight)
    stream = call(
        fine_kernel,
        jax.ShapeDtypeStruct((4, TOKENS, depth), BF16),
        [
            start, windows, fine_scale, own, left, right, up, down, gain,
            jnp.asarray(PLACES.T.copy()), jnp.asarray(PLACES[:OWN].copy()), *own_heads, fine_qkv, fine_out,
        ],
        (0, 1, 2),
        [pltpu.VMEM((KEYS - OWN, depth), F32)],
        flops=2 * KEYS * depth * 3 * depth,
        nbytes=5 * 2**20,
    )
    streams = gather_z(stream)
    split_w = gather_y(gather_x(after(chunk, up, down)))
    merge_w = after(merge_w, stream)
    block = merge_w.shape[2]
    bottom = call(
        merge_kernel,
        jax.ShapeDtypeStruct((NX, TOKENS, block), BF16),
        [place, *streams, merge_w, swap_core(merge_w)],
        (0,),
        [pltpu.VMEM((4 * depth, block), BF16)],
        flops=2 * OWN * 4 * depth * block,
        nbytes=3 * 2**20,
    )
    battn = bottom_out.shape[0]
    group = battn // NX
    deep = bottom_qkv.shape[0]
    weight = after(bottom_qkv, bottom)
    at = lax.axis_index("z") * group
    picked = [
        lax.dynamic_slice_in_dim(weight, part * battn + at, group, 1) for part in (1, 2, 0)
    ]
    qkv_w = jnp.concatenate(picked + [jnp.zeros((deep, 64), BF16)], axis=1)
    bfull, query, pairs = call(
        project_kernel,
        (
            jax.ShapeDtypeStruct((OWN, deep), BF16),
            jax.ShapeDtypeStruct((OWN, 256), F32),
            jax.ShapeDtypeStruct((16, OWN, 2 * group), BF16),
        ),
        [place, *gather_z(bottom), qkv_w],
        (0,),
        [pltpu.VMEM((OWN, deep), F32)],
        flops=2 * OWN * deep * 640,
        nbytes=4 * 2**20,
    )
    pairs = after(pairs, *split_w)
    near = lax.all_to_all(pairs, REST, 0, 0).reshape(16 * OWN, 2 * group)
    far = swap_core(near)
    near_part = call(
        near_kernel,
        (
            jax.ShapeDtypeStruct((3 * OWN, 1), F32),
            jax.ShapeDtypeStruct((3 * OWN, 1), F32),
            jax.ShapeDtypeStruct((3 * OWN, 256), F32),
        ),
        [bottom_scale, place, query, near],
        (0, 1),
        flops=2 * 3 * OWN * 1536 * 256 * 3,
        nbytes=2 * 2**20,
    )
    batt = call(
        far_kernel,
        jax.ShapeDtypeStruct((OWN, group), BF16),
        [bottom_scale, place, query, far, *near_part],
        (0, 1),
        flops=2 * 3 * OWN * 1536 * 256 * 3,
        nbytes=2 * 2**20,
    )
    near_w = after(jnp.stack(split_w), near)
    split_w = call(
        arrange_kernel,
        jax.ShapeDtypeStruct((32, TOKENS, deep), BF16),
        [place, near_w, swap_core(near_w)],
        (0,),
    ).reshape(depth, deep)
    split = call(
        output_kernel,
        jax.ShapeDtypeStruct((NX, TOKENS, depth), BF16),
        [place, *gather_z(batt), bfull, bottom_out, split_w],
        (0,),
        flops=2 * OWN * deep * 2 * depth,
        nbytes=5 * 2**20,
    )
    mixed = call(
        mix_kernel,
        jax.ShapeDtypeStruct((width, height, depth), BF16),
        [place, stream, *scatter_z(split), skip_mix[None]],
        (0,),
        [pltpu.VMEM((4, TOKENS, depth), F32)],
        flops=2 * 128 * 96 * depth,
        nbytes=2**20,
    )
    return mixed.transpose(1, 0, 2)


def solution(mesh):
    inner = Mesh(mesh.devices.reshape(4, 2, 2, 2, 4), ALL)
    placed = (
        P(GY, GX, None),
        P(),
        P(),
        P(),
        P(),
        P(),
        P(),
        P(),
        P(ALL, None),
        P(),
        P(),
        P(),
        P(None, ALL),
        P(),
    )
    return jax.shard_map(
        shards, mesh=inner, in_specs=placed, out_specs=P(GY, GX, None), check_vma=False
    )
```

```python
import math

import jax
import jax.numpy as jnp
import numpy as np
from jax import lax
from jax.experimental import pallas as pl
from jax.experimental.pallas import tpu as pltpu
from jax.sharding import Mesh, PartitionSpec as P

HEAD_DIM = 64
WIN = 7
REACH = WIN // 2
EPS = 1e-06
ROWS, COLS = 8, 12
OWN = ROWS * COLS
TOKENS = OWN // 4
KEYS = 256
FAR = 1000
BF16 = jnp.bfloat16
F32 = jnp.float32

ALL = ("z", "yl", "c", "yh", "x")
GY = ("z", "yl", "c")
GX = ("yh", "x")
REST = ("yl", "yh", "x")
NX = 4

VMEM_LIMIT = 40 * 2**20


def key_places():
    places = []
    for cols in (range(COLS), range(-REACH, 0), range(COLS, COLS + REACH)):
        places += [(r, c) for c in cols for r in range(ROWS)]
    for rows in (range(-REACH, 0), range(ROWS, ROWS + REACH)):
        places += [(r, c) for c in range(-REACH, COLS + REACH) for r in rows]
    places += [(FAR, FAR)] * (KEYS - len(places))
    return np.array(places, np.int32)


PLACES = key_places()


def reorder(flip):
    m = lax.broadcasted_iota(jnp.int32, (OWN, OWN), 1 if flip else 0)
    n = lax.broadcasted_iota(jnp.int32, (OWN, OWN), 0 if flip else 1)
    s = (m >= TOKENS).astype(jnp.int32) + (m >= 2 * TOKENS) + (m >= 3 * TOKENS)
    t = m - s * TOKENS
    source = (2 * (t // 4) + s % 2) * ROWS + 2 * (t % 4) + s // 2
    return (n == source).astype(F32).astype(BF16)


def block_ones():
    row = lax.broadcasted_iota(jnp.int32, (256, 256), 0) // HEAD_DIM
    col = lax.broadcasted_iota(jnp.int32, (256, 256), 1) // HEAD_DIM
    return (row == col).astype(F32).astype(BF16)


def dot(a, b):
    return jnp.dot(a, b, preferred_element_type=F32)


def dot_t(a, b):
    return lax.dot_general(a, b, (((1,), (1,)), ((), ())), preferred_element_type=F32)


def split_hi_lo(values):
    hi = values.astype(BF16)
    lo = (values - hi.astype(F32)).astype(BF16)
    return hi, lo


def unit_quad(values, ones):
    hi, lo = split_hi_lo(values * values)
    total = dot(hi, ones) + dot(lo, ones)
    return values * lax.rsqrt(total + EPS)


def full(shape):
    return pl.BlockSpec(memory_space=pltpu.VMEM)


def smem():
    return pl.BlockSpec(memory_space=pltpu.SMEM)


def call(body, out_shape, args, in_smem, scratch=(), flops=0, nbytes=0):
    return pl.pallas_call(
        body,
        out_shape=out_shape,
        in_specs=[smem() if i in in_smem else full(None) for i in range(len(args))],
        out_specs=jax.tree.map(lambda _: full(None), out_shape),
        scratch_shapes=list(scratch),
        compiler_params=pltpu.CompilerParams(vmem_limit_bytes=VMEM_LIMIT),
        cost_estimate=pl.CostEstimate(flops=flops, bytes_accessed=nbytes, transcendentals=0),
    )(*args)


def gain_kernel(step, row, freqs, gain):
    angles = step[0].astype(F32) * freqs[...]
    features = jnp.concatenate([jnp.cos(angles), jnp.sin(angles)], axis=1)
    gain[...] = 1.0 + 0.5 * (row[...].astype(F32) + features)


def normalise(x, gain):
    mean = jnp.mean(x * x, axis=-1, keepdims=True)
    return (x * lax.rsqrt(mean + EPS) * gain).astype(BF16)


def own_kernel(own, gain, qkv, out_w, query, key, value):
    width = own.shape[2]
    ones = block_ones()
    tokens = normalise(own[...].astype(F32).reshape(OWN, width), gain[...])
    for at in range(0, width, 256):
        here = slice(at, at + 256)
        query[:, here] = unit_quad(dot(tokens, qkv[:, here]), ones)
        part = dot(tokens, qkv[:, width + at : width + at + 256])
        key[:, here] = unit_quad(part, ones).astype(BF16)
        value[:, here] = dot(tokens, qkv[:, 2 * width + at : 2 * width + at + 256]).astype(BF16)


def fine_kernel(
    start, windows, scales, own, left, right, up, down, gain, key_place, query_place,
    own_query, own_key, own_value, qkv, out_w, stream, tokens,
):
    width = own.shape[2]
    tokens[KEYS - OWN - 8 :] = jnp.zeros((8, width), F32)
    at = 0
    for strip in (left, right):
        tokens[at : at + REACH * ROWS] = strip[...].astype(F32).reshape(REACH * ROWS, width)
        at += REACH * ROWS
    for strip in (up, down):
        for c in range(strip.shape[0]):
            tokens[at : at + REACH] = strip[c].astype(F32)
            at += REACH
    halo = normalise(tokens[...], gain[...])
    row_k, col_k = key_place[0:1, :], key_place[1:2, :]
    row_q, col_q = query_place[:, 0:1], query_place[:, 1:2]
    row_g, col_g = row_k + start[0], col_k + start[1]
    inside = (row_g >= 0) & (row_g < start[2]) & (col_g >= 0) & (col_g < start[3])
    apart = jnp.maximum(jnp.abs(row_k - row_q), jnp.abs(col_k - col_q))
    apart = jnp.where(inside, apart, FAR)

    ones = block_ones()
    lane = lax.broadcasted_iota(jnp.int32, (OWN, 256), 1) // HEAD_DIM
    update = own[...].astype(F32).reshape(OWN, width)
    for quad in range(width // 256):
        at = quad * 256
        query = own_query[:, at : at + 256]
        key = unit_quad(dot(halo, qkv[:, width + at : width + at + 256]), ones).astype(BF16)
        key = jnp.concatenate([own_key[:, at : at + 256], key], axis=0)
        value = dot(halo, qkv[:, 2 * width + at : 2 * width + at + 256]).astype(BF16)
        value = jnp.concatenate([own_value[:, at : at + 256], value], axis=0)
        hi, lo = split_hi_lo(query)
        rows = [jnp.where(lane == h, hi, 0) for h in range(4)]
        rows += [jnp.where(lane == h, lo, 0) for h in range(4)]
        score = dot_t(jnp.concatenate(rows, axis=0), key)
        score = score[: 4 * OWN] + score[4 * OWN :]
        weights, totals = [], []
        for h in range(4):
            head = quad * 4 + h
            radius = (windows[head] - 1) // 2
            part = scales[head] * score[h * OWN : (h + 1) * OWN]
            part = jnp.where(apart <= radius, part, -jnp.inf)
            part = jnp.exp(part - jnp.max(part, axis=-1, keepdims=True))
            totals.append(jnp.sum(part, axis=-1, keepdims=True))
            weights.append(part.astype(BF16))
        mixed = dot(jnp.concatenate(weights, axis=0), value)
        att = jnp.zeros((OWN, 256), F32)
        for h in range(4):
            att = jnp.where(lane == h, mixed[h * OWN : (h + 1) * OWN] / totals[h], att)
        update = update + dot(att.astype(BF16), out_w[at : at + 256, :])
    result = dot(reorder(False), update.astype(BF16))
    for s in range(4):
        stream[s] = result[s * TOKENS : (s + 1) * TOKENS].astype(BF16)


def merge_kernel(place, p0, p1, p2, p3, mine, other, bottom, weight):
    width = p0.shape[2]
    half = mine.shape[0] * mine.shape[1] // 8
    for i in range(8):
        for ref, core in ((mine, place[1]), (other, 1 - place[1])):
            at = pl.multiple_of(i * 2 * half + core * half, half)
            weight[pl.ds(at, half), :] = ref[i * 8 : i * 8 + 8].reshape(half, ref.shape[2])
    acc = None
    for s in range(4):
        rows = jnp.concatenate([p[s].astype(F32) for p in (p0, p1, p2, p3)], axis=0).astype(BF16)
        term = dot(rows, weight[s * width : (s + 1) * width, :])
        acc = term if acc is None else acc + term
    for k in range(NX):
        bottom[lax.rem(place[0] + NX - k, NX)] = acc[k * TOKENS : (k + 1) * TOKENS].astype(BF16)


def project_kernel(place, p0, p1, p2, p3, weight, bottom, query, pairs, whole):
    block = p0.shape[2]
    ones = block_ones()
    for k, p in enumerate((p0, p1, p2, p3)):
        at = pl.multiple_of(lax.rem(place[0] + NX - k, NX) * block, 128)
        rows = jnp.concatenate([p[i].astype(F32) for i in range(NX)], axis=0)
        whole[:, pl.ds(at, block)] = rows
    x = whole[...]
    bottom[...] = x.astype(BF16)
    mean = jnp.mean(x * x, axis=-1, keepdims=True)
    normed = (x * lax.rsqrt(mean + EPS)).astype(BF16)
    proj = dot(normed, weight[...])
    first = proj[:, :256]
    lane = lax.broadcasted_iota(jnp.int32, first.shape, 1)
    first = jnp.where(lane < 192, unit_quad(first, ones), first)
    kv = jnp.concatenate([first, proj[:, 256:384]], axis=1).astype(BF16)
    for i in range(pairs.shape[0]):
        pairs[i] = kv
    query[...] = unit_quad(proj[:, 384:640], ones)


def attend_part(scales, place, query, ref):
    lane = lax.broadcasted_iota(jnp.int32, query.shape, 1) // HEAD_DIM
    count = query.shape[0]
    hi, lo = split_hi_lo(query[...])
    rows = [jnp.where(lane == h, hi, 0) for h in range(3)]
    rows += [jnp.where(lane == h, lo, 0) for h in range(3)]
    scale = jnp.concatenate(
        [jnp.full((count, 1), scales[3 * place[0] + h], F32) for h in range(3)], axis=0
    )
    score = dot_t(jnp.concatenate(rows, axis=0), ref[:, :256])
    score = scale * (score[: 3 * count] + score[3 * count :])
    highest = jnp.max(score, axis=-1, keepdims=True)
    part = jnp.exp(score - highest)
    total = jnp.sum(part, axis=-1, keepdims=True)
    return highest, total, dot(part.astype(BF16), ref[:, 128:384])


def near_kernel(scales, place, query, near, highest, total, acc):
    highest[...], total[...], acc[...] = attend_part(scales, place, query, near)


def far_kernel(scales, place, query, far, near_highest, near_total, near_acc, out):
    count = query.shape[0]
    highest, total, acc = attend_part(scales, place, query, far)
    top = jnp.maximum(highest, near_highest[...])
    fade, near_fade = jnp.exp(highest - top), jnp.exp(near_highest[...] - top)
    acc = acc * fade + near_acc[...] * near_fade
    acc = acc / (total * fade + near_total[...] * near_fade)
    lane = lax.broadcasted_iota(jnp.int32, query.shape, 1) // HEAD_DIM
    att = jnp.zeros((count, 256), F32)
    for h in range(3):
        att = jnp.where(lane == h + 1, acc[h * count : (h + 1) * count], att)
    out[...] = att[:, 64:].astype(BF16)


def arrange_kernel(place, mine, other, weight):
    for ref, core in ((mine, place[1]), (other, 1 - place[1])):
        for step in range(4):
            yl = place[2] if step < 2 else 1 - place[2]
            yh = place[3] if step % 2 == 0 else 1 - place[3]
            for k in range(4):
                x = lax.rem(place[4] + 4 - k, 4)
                weight[(yl * 2 + core) * 8 + yh * 4 + x] = ref[step, k]


def output_kernel(place, p0, p1, p2, p3, bottom, out_w, split_w, split):
    acc = bottom[...].astype(F32)
    block = p0.shape[1]
    for k, p in enumerate((p0, p1, p2, p3)):
        at = pl.multiple_of(lax.rem(place[0] + NX - k, NX) * block, 64)
        acc = acc + dot(p[...], out_w[pl.ds(at, block), :])
    result = dot_t(acc.astype(BF16), split_w[...])
    for i in range(NX):
        split[i] = result[i * TOKENS : (i + 1) * TOKENS].astype(BF16)


def mix_kernel(place, stream, u0, u1, u2, u3, mix, out, upward):
    for k, u in enumerate((u0, u1, u2, u3)):
        upward[lax.rem(place[0] + NX - k, NX)] = u[...].astype(F32)
    s = jnp.concatenate([stream[i].astype(F32) for i in range(4)], axis=0)
    u = upward[...].reshape(OWN, out.shape[2])
    mixed = (s + mix[...] * (u - s)).astype(BF16)
    grid = dot(reorder(True), mixed)
    out[...] = grid.reshape(out.shape).astype(BF16)


def shift(x, axis, size, step):
    return lax.ppermute(x, axis, [(i, i + step) for i in range(size) if 0 <= i + step < size])


def gather_z(x):
    return [x] + [
        lax.ppermute(x, "z", [(i, (i + s) % NX) for i in range(NX)]) for s in range(1, NX)
    ]


def scatter_z(x):
    z = lax.axis_index("z")
    parts = [lax.dynamic_index_in_dim(x, (z + s) % NX, 0, keepdims=False) for s in range(NX)]
    return parts[:1] + [
        lax.ppermute(parts[s], "z", [(i, (i + s) % NX) for i in range(NX)]) for s in range(1, NX)
    ]


def swap_core(x):
    return lax.ppermute(x, "c", [(0, 1), (1, 0)])


def after(x, *others):
    return lax.optimization_barrier((x, *others))[0]


def merge_columns(merge_weight):
    rows, width = merge_weight.shape
    block = width // NX
    parts = jnp.stack([merge_weight[:, i * block : (i + 1) * block] for i in range(NX)])
    parts = jnp.broadcast_to(parts[:, None], (NX, 16, rows, block)).reshape(16 * NX, rows, block)
    return lax.all_to_all(parts, ("z", *REST), 0, 0)


def gather_x(x):
    return jnp.stack(
        [x] + [lax.ppermute(x, "x", [(i, (i + s) % 4) for i in range(4)]) for s in range(1, 4)]
    )


def gather_y(x):
    return [x] + [
        lax.ppermute(x, ("yl", "yh"), [(i, i ^ s) for i in range(4)]) for s in range(1, 4)
    ]


def shards(
    fine,
    class_table,
    label,
    timestep,
    windows,
    fine_scale,
    fine_qkv,
    fine_out,
    merge_weight,
    bottom_scale,
    bottom_qkv,
    bottom_out,
    split_weight,
    skip_mix,
):
    height, width, depth = fine.shape
    own = fine.transpose(1, 0, 2)
    left = shift(own[width - REACH :], GX, 8, 1)
    right = shift(own[:REACH], GX, 8, -1)
    wide = jnp.concatenate([left, own, right], axis=0)
    row = lax.dynamic_slice_in_dim(class_table, label[0], 1, 0)
    half = depth // 2
    freqs = np.exp(np.float32(-math.log(10000.0)) * np.arange(half, dtype=np.float32) / half)
    gain = call(
        gain_kernel,
        jax.ShapeDtypeStruct((1, depth), F32),
        [timestep, row, jnp.asarray(freqs[None], F32)],
        (0,),
    )
    own_heads = call(
        own_kernel,
        (
            jax.ShapeDtypeStruct((OWN, depth), F32),
            jax.ShapeDtypeStruct((OWN, depth), BF16),
            jax.ShapeDtypeStruct((OWN, depth), BF16),
        ),
        [own, gain, fine_qkv, fine_out],
        (),
        flops=2 * OWN * depth * 3 * depth,
        nbytes=5 * 2**20,
    )
    chunk = split_weight.T
    wide = after(wide, chunk, *own_heads)
    up = shift(wide[:, height - REACH :], GY, 16, 1)
    down = shift(wide[:, :REACH], GY, 16, -1)
    start = jnp.stack(
        [
            lax.axis_index(GY) * height,
            lax.axis_index(GX) * width,
            jnp.int32(16 * height),
            jnp.int32(8 * width),
        ]
    ).astype(jnp.int32)
    place = jnp.stack([lax.axis_index(name) for name in ("z", "c", "yl", "yh", "x")])
    place = place.astype(jnp.int32)

    merge_w = merge_columns(merge_weight)
    stream = call(
        fine_kernel,
        jax.ShapeDtypeStruct((4, TOKENS, depth), BF16),
        [
            start, windows, fine_scale, own, left, right, up, down, gain,
            jnp.asarray(PLACES.T.copy()), jnp.asarray(PLACES[:OWN].copy()), *own_heads, fine_qkv, fine_out,
        ],
        (0, 1, 2),
        [pltpu.VMEM((KEYS - OWN, depth), F32)],
        flops=2 * KEYS * depth * 3 * depth,
        nbytes=5 * 2**20,
    )
    streams = gather_z(stream)
    split_w = gather_y(gather_x(after(chunk, up, down)))
    merge_w = after(merge_w, stream)
    block = merge_w.shape[2]
    bottom = call(
        merge_kernel,
        jax.ShapeDtypeStruct((NX, TOKENS, block), BF16),
        [place, *streams, merge_w, swap_core(merge_w)],
        (0,),
        [pltpu.VMEM((4 * depth, block), BF16)],
        flops=2 * OWN * 4 * depth * block,
        nbytes=3 * 2**20,
    )
    battn = bottom_out.shape[0]
    group = battn // NX
    deep = bottom_qkv.shape[0]
    weight = after(bottom_qkv, bottom)
    at = lax.axis_index("z") * group
    picked = [
        lax.dynamic_slice_in_dim(weight, part * battn + at, group, 1) for part in (1, 2, 0)
    ]
    qkv_w = jnp.concatenate(picked + [jnp.zeros((deep, 64), BF16)], axis=1)
    bfull, query, pairs = call(
        project_kernel,
        (
            jax.ShapeDtypeStruct((OWN, deep), BF16),
            jax.ShapeDtypeStruct((OWN, 256), F32),
            jax.ShapeDtypeStruct((16, OWN, 2 * group), BF16),
        ),
        [place, *gather_z(bottom), qkv_w],
        (0,),
        [pltpu.VMEM((OWN, deep), F32)],
        flops=2 * OWN * deep * 640,
        nbytes=4 * 2**20,
    )
    near = lax.all_to_all(pairs, REST, 0, 0).reshape(16 * OWN, 2 * group)
    far = swap_core(near)
    near_part = call(
        near_kernel,
        (
            jax.ShapeDtypeStruct((3 * OWN, 1), F32),
            jax.ShapeDtypeStruct((3 * OWN, 1), F32),
            jax.ShapeDtypeStruct((3 * OWN, 256), F32),
        ),
        [bottom_scale, place, query, near],
        (0, 1),
        flops=2 * 3 * OWN * 1536 * 256 * 3,
        nbytes=2 * 2**20,
    )
    batt = call(
        far_kernel,
        jax.ShapeDtypeStruct((OWN, group), BF16),
        [bottom_scale, place, query, far, *near_part],
        (0, 1),
        flops=2 * 3 * OWN * 1536 * 256 * 3,
        nbytes=2 * 2**20,
    )
    near_w = after(jnp.stack(split_w), near)
    split_w = call(
        arrange_kernel,
        jax.ShapeDtypeStruct((32, TOKENS, deep), BF16),
        [place, near_w, swap_core(near_w)],
        (0,),
    ).reshape(depth, deep)
    split = call(
        output_kernel,
        jax.ShapeDtypeStruct((NX, TOKENS, depth), BF16),
        [place, *gather_z(batt), bfull, bottom_out, split_w],
        (0,),
        flops=2 * OWN * deep * 2 * depth,
        nbytes=5 * 2**20,
    )
    mixed = call(
        mix_kernel,
        jax.ShapeDtypeStruct((width, height, depth), BF16),
        [place, stream, *scatter_z(split), skip_mix[None]],
        (0,),
        [pltpu.VMEM((4, TOKENS, depth), F32)],
        flops=2 * 128 * 96 * depth,
        nbytes=2**20,
    )
    return mixed.transpose(1, 0, 2)


def solution(mesh):
    inner = Mesh(mesh.devices.reshape(4, 2, 2, 2, 4), ALL)
    placed = (
        P(GY, GX, None),
        P(),
        P(),
        P(),
        P(),
        P(),
        P(),
        P(),
        P(ALL, None),
        P(),
        P(),
        P(),
        P(None, ALL),
        P(),
    )
    return jax.shard_map(
        shards, mesh=inner, in_specs=placed, out_specs=P(GY, GX, None), check_vma=False
    )
```
